256 devices in a mesh: slab: 32 (over y, z), narrow: 8 (over x, core).
Axes of the slice: x: 4, y: 4, z: 8, core: 2. Of those that a mesh axis runs over, the one named last changes fastest.
Arguments:
- rhs: float32 [128, 128, 16, 256], P('slab', 'narrow'), may hold values from -6 to 6
- skeleton_matrix_fine: float32 [24, 40], replicated, may hold values from -0.5 to 0.5
- elimination_inverse_fine: float32 [40, 40], replicated, may hold values from -1 to 1
- schur_update_fine: float32 [27, 24, 40], replicated, may hold values from -0.109375 to 0.109375
- skeleton_matrix_mid: float32 [48, 144], replicated, may hold values from -0.3125 to 0.3125
- elimination_inverse_mid: float32 [144, 144], replicated, may hold values from -0.5 to 0.5
- schur_update_mid: float32 [27, 48, 144], replicated, may hold values from -0.0546875 to 0.0546875
- skeleton_matrix_coarse: float32 [96, 288], replicated, may hold values from -0.21875 to 0.21875
- elimination_inverse_coarse: float32 [288, 288], replicated, may hold values from -0.375 to 0.375
- schur_update_coarse: float32 [27, 96, 288], replicated, may hold values from -0.0390625 to 0.0390625
Outputs:
- solved1: float32 [128, 128, 16, 160], P('slab', 'narrow')
- solved2: float32 [64, 64, 8, 576], P('slab', 'narrow')
- solved3: float32 [32, 32, 4, 1152], P('slab', 'narrow')
- coarse_rhs: float32 [32, 32, 4, 384], P('slab')
The draws below stay inside these ranges and needn't reach their ends.
All inputs are finite; a program needn't handle non-finite values.
Results may differ from the reference program's by a relative error of at most 0.0001.
Values sent between devices are 32-bit elements; how exact they have to be, the bound alone decides.
No kernel may reach another device: no remote copies, remote signals or barrier semaphores. Data moves between devices by JAX's collectives and lax.ppermute only.
A program may use at most 256 MiB of HBM per device.

```python
import jax
import jax.numpy as jnp
from jax import lax

Q1 = 64
SKELETON_FINE = 24
SKELETON_MID = 48
SKELETON_COARSE = 96
RHS = 4
BZD = 16
REDUNDANT_FINE = 40
REDUNDANT_MID = 144
REDUNDANT_COARSE = 288
BX = 128
BY = 128


def steps_of(rng, dims, shards, smallest, largest):
    def one(position, shards_of):
        steps = jax.random.uniform(jax.random.fold_in(jax.random.fold_in(rng, 6), position), (shards_of,), jnp.float32, smallest / len(shards), largest / len(shards))
        return jnp.repeat(jnp.exp(steps), dims[position] // shards_of).reshape((-1,) + (1,) * (len(dims) - position - 1))

    level = one(*shards[0])
    for cut in shards[1:]:
        level = level * one(*cut)
    return level


def centred(rng, shape, spread, most, split=(), held_as=jnp.bfloat16):
    factor_of = steps_of(rng, shape, split, -0.22, 0.18) if split else 1.0
    entries = jax.random.normal(rng, shape, jnp.float32) * spread * factor_of
    return jnp.minimum(jnp.maximum(entries, -most), most).astype(held_as)


def setup_inputs(seed: int = 0) -> dict:
    keys = jax.random.split(jax.random.key(seed), 11)
    rhs = centred(keys[0], (BX, BY, BZD, Q1 * RHS), 1.0, 6.0, ((0, 32), (1, 8)), jnp.float32)
    skeleton_matrix_fine = centred(keys[1], (SKELETON_FINE, REDUNDANT_FINE), (3 * REDUNDANT_FINE) ** -0.5, 0.5, (), jnp.float32)
    elimination_inverse_fine = centred(keys[2], (REDUNDANT_FINE, REDUNDANT_FINE), REDUNDANT_FINE ** -0.5, 1.0, (), jnp.float32)
    schur_update_fine = centred(keys[3], (27, SKELETON_FINE, REDUNDANT_FINE), (81 * REDUNDANT_FINE) ** -0.5, 0.109375, (), jnp.float32)
    skeleton_matrix_mid = centred(keys[4], (SKELETON_MID, REDUNDANT_MID), (3 * REDUNDANT_MID) ** -0.5, 0.3125, (), jnp.float32)
    elimination_inverse_mid = centred(keys[5], (REDUNDANT_MID, REDUNDANT_MID), REDUNDANT_MID ** -0.5, 0.5, (), jnp.float32)
    schur_update_mid = centred(keys[6], (27, SKELETON_MID, REDUNDANT_MID), (81 * REDUNDANT_MID) ** -0.5, 0.0546875, (), jnp.float32)
    skeleton_matrix_coarse = centred(keys[7], (SKELETON_COARSE, REDUNDANT_COARSE), (3 * REDUNDANT_COARSE) ** -0.5, 0.21875, (), jnp.float32)
    elimination_inverse_coarse = centred(keys[8], (REDUNDANT_COARSE, REDUNDANT_COARSE), REDUNDANT_COARSE ** -0.5, 0.375, (), jnp.float32)
    schur_update_coarse = centred(keys[9], (27, SKELETON_COARSE, REDUNDANT_COARSE), (81 * REDUNDANT_COARSE) ** -0.5, 0.0390625, (), jnp.float32)
    return {"rhs": rhs, "skeleton_matrix_fine": skeleton_matrix_fine, "elimination_inverse_fine": elimination_inverse_fine, "schur_update_fine": schur_update_fine, "skeleton_matrix_mid": skeleton_matrix_mid, "elimination_inverse_mid": elimination_inverse_mid, "schur_update_mid": schur_update_mid, "skeleton_matrix_coarse": skeleton_matrix_coarse, "elimination_inverse_coarse": elimination_inverse_coarse, "schur_update_coarse": schur_update_coarse}


def divide_tier(box_cells, skeleton_matrix, elimination_inverse, skeleton_part):
    shape = box_cells.shape
    vectors = box_cells.reshape(shape[0], shape[1], shape[2], -1, RHS)
    skeleton_entries = vectors[:, :, :, :skeleton_part, :]
    leftover_part = vectors[:, :, :, skeleton_part:, :]
    solution_vector = jnp.einsum('tl,sbale->sbate', elimination_inverse, leftover_part, precision=lax.Precision.HIGHEST)
    skeleton_entries = skeleton_entries - jnp.einsum('sr,xyzrk->xyzsk', skeleton_matrix, leftover_part, precision=lax.Precision.HIGHEST)
    return solution_vector, skeleton_entries


def apply_updates(skeleton_entries, padded, schur_update):
    sizes = skeleton_entries.shape
    for index in range(27):
        along_x = index // 9
        along_y = (index // 3) % 3
        along_z = index % 3
        window = padded[along_x:along_x + sizes[0], along_y:along_y + sizes[1], along_z:along_z + sizes[2]]
        skeleton_entries = skeleton_entries - jnp.einsum('sr,xyzrk->xyzsk', schur_update[index], window, precision=lax.Precision.HIGHEST)
    return skeleton_entries


def combine_offspring(skeleton_entries):
    sx, sy, sz, skeleton_part, count = skeleton_entries.shape
    grouped = skeleton_entries.reshape(sx // 2, 2, sy // 2, 2, sz // 2, 2, skeleton_part, count)
    grouped = grouped.transpose(0, 2, 4, 1, 3, 5, 6, 7)
    return grouped.reshape(sx // 2, sy // 2, sz // 2, 8 * skeleton_part * count)


def single_tier(box_cells, skeleton_matrix, elimination_inverse, schur_update, skeleton_part):
    solution_vector, skeleton_entries = divide_tier(box_cells, skeleton_matrix, elimination_inverse, skeleton_part)
    padded = jnp.pad(solution_vector, ((1, 1), (1, 1), (1, 1), (0, 0), (0, 0)))
    skeleton_entries = apply_updates(skeleton_entries, padded, schur_update)
    return solution_vector, skeleton_entries


def flatten(values):
    shape = values.shape
    return values.reshape(shape[0], shape[1], shape[2], -1)


def reference(rhs, skeleton_matrix_fine, elimination_inverse_fine, schur_update_fine, skeleton_matrix_mid, elimination_inverse_mid, schur_update_mid, skeleton_matrix_coarse, elimination_inverse_coarse, schur_update_coarse):
    solution_fine, skeleton_entries = single_tier(rhs, skeleton_matrix_fine, elimination_inverse_fine, schur_update_fine, SKELETON_FINE)
    solution_mid, skeleton_entries = single_tier(combine_offspring(skeleton_entries), skeleton_matrix_mid, elimination_inverse_mid, schur_update_mid, SKELETON_MID)
    solution_coarse, skeleton_entries = single_tier(combine_offspring(skeleton_entries), skeleton_matrix_coarse, elimination_inverse_coarse, schur_update_coarse, SKELETON_COARSE)
    return flatten(solution_fine), flatten(solution_mid), flatten(solution_coarse), flatten(skeleton_entries)
```

```python
import functools

import jax
import jax.numpy as jnp
from jax import lax
from jax.experimental import pallas as pl
from jax.experimental.pallas import tpu as pltpu
from jax.sharding import PartitionSpec as P

F32 = jnp.float32
BF16 = jnp.bfloat16
VMEM_LIMIT = 48 * 1024 * 1024


def dot(a, b):
    return lax.dot_general(a, b, (((1,), (0,)), ((), ())), preferred_element_type=F32)


def halves(x):
    high = x.astype(BF16)
    return high, (x - high.astype(F32)).astype(BF16)


def dot3(a_high, a_low, b):
    b_high, b_low = halves(b)
    return dot(a_high, b_high) + dot(a_low, b_high) + dot(a_high, b_low)


def lanes(shape):
    return lax.broadcasted_iota(jnp.int32, shape, len(shape) - 1)


def roll(x, shift):
    size = x.shape[1]
    shift = shift % size
    return x if shift == 0 else pltpu.roll(x, shift, 1)


def stacked(x):
    high = x.astype(BF16).astype(F32)
    zeros = jnp.zeros((8, x.shape[1]), F32)
    return jnp.concatenate([high, high, x - high, zeros], axis=0).astype(BF16)


def packed_left(ref, block, x):
    high = x.astype(BF16).astype(F32)
    base = block * 128
    ref[:, base : base + 40] = high
    ref[:, base + 40 : base + 80] = x - high
    ref[:, base + 80 : base + 120] = high


def to_partners(even, upward, downward):
    return jnp.where(even, upward, downward), jnp.where(even, downward, upward)


def from_partners(index, count, first, second):
    even = index % 2 == 0
    above = jnp.where(even, first, second)
    below = jnp.where(even, second, first)
    zeros = jnp.zeros_like(above)
    return jnp.where(index < count - 1, above, zeros), jnp.where(index > 0, below, zeros)


def fine_kernel(
    place, rhs, skel, elim, update, solved, skeleton, inner, edge, send_a, send_b,
    left_c, left_u, turned, cat, out_rows,
):
    left_c[...] = jnp.zeros_like(left_c)
    left_u[...] = jnp.zeros_like(left_u)
    packed_left(left_c, 0, jnp.concatenate([elim[...], skel[...]], axis=0))
    for dx in range(3):
        packed_left(left_u, dx, update[dx * 216 : (dx + 1) * 216, :])
    solve = left_c[...].astype(BF16)
    for x in range(4):
        for part in range(2):
            turned[part] = rhs[x * 256 + part * 128 : x * 256 + (part + 1) * 128, :].T
        for k in range(4):
            vector = jnp.concatenate(
                [turned[part, pl.ds(k, 64, stride=4), :] for part in range(2)], axis=1
            )
            product = dot(solve, stacked(vector[24:64]))
            skeleton[x, :, k * 256 : (k + 1) * 256] = vector[:24] - product[40:64]
            solution_vector = product[:40]
            cat[k, x] = stacked(solution_vector)
            for part in range(2):
                out_rows[part, pl.ds(k, 40, stride=4), :] = solution_vector[
                    :, part * 128 : (part + 1) * 128
                ]
        for part in range(2):
            solved[x * 256 + part * 128 : x * 256 + (part + 1) * 128, :] = out_rows[part].T

    operator = left_u[...].astype(BF16)
    lane = lanes((24, 256))
    z = lane % 16
    half = lanes((24, 128))
    low = [jnp.zeros((24, 128), F32)] * 3
    high = [jnp.zeros((24, 128), F32)] * 3
    for k in range(4):
        for c in range(6):
            first = max(0, c - 2)
            last = min(3, c)
            columns = operator[:, (first - c + 2) * 128 : (last - c + 3) * 128]
            right = cat[k, first : last + 1].reshape((last + 1 - first) * 128, 256)
            product = dot(columns, right)
            sums = []
            for dy in range(3):
                parts = [product[(dy * 3 + dz) * 24 : (dy * 3 + dz + 1) * 24] for dz in range(3)]
                sums.append(
                    parts[1]
                    + jnp.where(z > 0, roll(parts[0], 1), 0.0)
                    + jnp.where(z < 15, roll(parts[2], -1), 0.0)
                )
            from_below = roll(sums[0], 16)
            from_above = roll(sums[2], -16)
            total = (
                sums[1]
                + jnp.where(lane >= 16, from_below, 0.0)
                + jnp.where(lane < 240, from_above, 0.0)
            )
            here = slice(k * 256, (k + 1) * 256)
            if c == 0:
                edge[0, :, here] = total
            elif c == 5:
                edge[1, :, here] = total
            else:
                inner[c - 1, :, here] = total
            slot = k * 6 + c
            q, u = slot // 8, slot % 8
            border = roll(jnp.where(half >= 112, from_above[:, 128:], from_below[:, :128]), 16 * u)
            high[q] = jnp.where(half // 16 == u, border, high[q])
            low[q] = jnp.where(half // 16 == (u + 7) % 8, border, low[q])
    even = place[1] % 2 == 0
    for q in range(3):
        here = slice(q * 128, (q + 1) * 128)
        send_a[:, here], send_b[:, here] = to_partners(even, high[q], low[q])


def fine_border(above, below, slot):
    half = lanes((24, 128))
    q, u = slot // 8, slot % 8
    here = slice(q * 128, (q + 1) * 128)
    start = jnp.where(half < 16, roll(below[:, here], -16 * u), 0.0)
    end = jnp.where(half >= 112, roll(above[:, here], -16 * u), 0.0)
    return start, end


def fine_edge_kernel(narrow, place, edge, got_a, got_b, send_a, send_b):
    above, below = from_partners(place[1], narrow, got_a[...], got_b[...])
    even = place[0] % 2 == 0
    for k in range(4):
        planes = []
        for side, c in ((0, 0), (1, 5)):
            start, end = fine_border(above, below, k * 6 + c)
            planes.append(
                (
                    edge[side, :, k * 256 : k * 256 + 128] + start,
                    edge[side, :, k * 256 + 128 : (k + 1) * 256] + end,
                )
            )
        for part in range(2):
            here = slice(k * 256 + part * 128, k * 256 + (part + 1) * 128)
            send_a[:, here], send_b[:, here] = to_partners(even, planes[1][part], planes[0][part])


def operators_kernel(
    skel2, elim2, update2, skel3, elim3, update3,
    solve2_h, solve2_l, update2_h, update2_l, solve3_h, solve3_l, update3_h, update3_l, sort2, sort3,
):
    solve2_h[...], solve2_l[...] = halves(jnp.concatenate([elim2[...], skel2[...]], axis=0))
    update2_h[...], update2_l[...] = halves(update2[...])
    solve3_h[...], solve3_l[...] = halves(jnp.concatenate([elim3[...], skel3[...]], axis=0))
    update3_h[...], update3_l[...] = halves(update3[...])
    row = lax.broadcasted_iota(jnp.int32, (256, 256), 0)
    y, z = row // 16, row % 16
    goal = ((y % 2) * 2 + z % 2) * 64 + (y // 2) * 8 + z // 2
    sort2[...] = jnp.where(goal == lanes((256, 256)), 1.0, 0.0).astype(BF16)
    row = lax.broadcasted_iota(jnp.int32, (128, 256), 0)
    x, y, z = row // 64, row // 8 % 8, row % 8
    goal = ((x * 2 + y % 2) * 2 + z % 2) * 32 + (y // 2 + 2) * 4 + z // 2
    sort3[...] = jnp.where(goal == lanes((128, 256)), 1.0, 0.0).astype(BF16)


def mid_kernel(
    slabs, narrow, place, skeleton1, inner1, got_a, got_b, plane_a, plane_b, sort,
    solve_h, solve_l, update_h, update_l,
    solved, skeleton, inner, edge, send_a, send_b,
    parts, vector, product, out_rows,
):
    above, below = from_partners(place[1], narrow, got_a[...], got_b[...])
    plane_above, plane_below = from_partners(place[0], slabs, plane_a[...], plane_b[...])
    for k in range(4):
        for x in range(4):
            start, end = fine_border(above, below, k * 6 + x + 1)
            here = slice(k * 256, (k + 1) * 256)
            value = (
                skeleton1[x, :, here] - inner1[x, :, here] - jnp.concatenate([start, end], axis=1)
            )
            if x == 0:
                value = value - plane_below[:, here]
            if x == 3:
                value = value - plane_above[:, here]
            top = value.astype(BF16).astype(F32)
            parts[k * 4 + x] = jnp.concatenate([top, value - top], axis=0).astype(BF16)
    arranged = dot(parts[...].reshape(16 * 48, 256), sort[...])
    half = lanes((24, 128))
    for k in range(4):
        for dx in range(2):
            pair = []
            for x in (dx, 2 + dx):
                base = (k * 4 + x) * 48
                pair.append(arranged[base : base + 24] + arranged[base + 24 : base + 48])
            for dy in range(2):
                first, second = [v[:, dy * 128 : (dy + 1) * 128] for v in pair]
                here = slice(k * 128, (k + 1) * 128)
                child = (dx * 2 + dy) * 2
                vector[child * 24 : child * 24 + 24, here] = jnp.where(
                    half < 64, first, roll(second, 64)
                )
                vector[child * 24 + 24 : child * 24 + 48, here] = jnp.where(
                    half < 64, roll(first, 64), second
                )
    result = dot3(solve_h[...], solve_l[...], vector[48:, :])
    solution_vector = result[:144]
    skeleton[...] = vector[:48, :] - result[144:]
    for k in range(4):
        out_rows[pl.ds(k, 144, stride=4), :] = solution_vector[:, k * 128 : (k + 1) * 128]
    product[...] = dot3(update_h[...], update_l[...], solution_vector)
    solved[...] = out_rows[...].T

    lane = lanes((48, 128))
    i, j, l = lane // 64, lane // 8 % 8, lane % 8
    low = jnp.zeros((48, 128), F32)
    high = jnp.zeros((48, 128), F32)
    for k in range(4):
        here = slice(k * 128, (k + 1) * 128)
        totals, borders = [], []
        for dx in range(3):
            sums = []
            for dy in range(3):
                base = (dx * 9 + dy * 3) * 48
                terms = [product[base + dz * 48 : base + (dz + 1) * 48, here] for dz in range(3)]
                sums.append(
                    terms[1]
                    + jnp.where(l > 0, roll(terms[0], 1), 0.0)
                    + jnp.where(l < 7, roll(terms[2], -1), 0.0)
                )
            from_below = roll(sums[0], 8)
            from_above = roll(sums[2], -8)
            totals.append(
                sums[1] + jnp.where(j > 0, from_below, 0.0) + jnp.where(j < 7, from_above, 0.0)
            )
            borders.append(roll(jnp.where(j == 7, from_above, from_below), 64))
        for kind, (minus, zero, plus) in enumerate((totals, borders)):
            inside = zero + jnp.where(i == 0, roll(plus, 64), roll(minus, 64))
            outside = jnp.where(i == 0, plus, minus)
            if kind == 0:
                inner[:, here] = inside
                edge[:, here] = outside
            else:
                for a, value in enumerate((inside, outside)):
                    u = k * 2 + a
                    moved = roll(value, 8 * u)
                    high = jnp.where(j == u, moved, high)
                    low = jnp.where(j == (u + 7) % 8, moved, low)
    send_a[...], send_b[...] = to_partners(place[1] % 2 == 0, high, low)


def mid_border(above, below, u):
    j = lanes((48, 128)) // 8 % 8
    return jnp.where(j == 0, roll(below, -8 * u), 0.0) + jnp.where(j == 7, roll(above, -8 * u), 0.0)


def mid_edge_kernel(narrow, place, edge, got_a, got_b, send_a, send_b):
    above, below = from_partners(place[1], narrow, got_a[...], got_b[...])
    even = place[0] % 2 == 0
    half = lanes((48, 128))
    for p in range(2):
        pair = []
        for k in (2 * p, 2 * p + 1):
            pair.append(edge[:, k * 128 : (k + 1) * 128] + mid_border(above, below, k * 2 + 1))
        moved = roll(pair[0], 64)
        low = jnp.where(half >= 64, moved, pair[1])
        high = jnp.where(half < 64, moved, pair[1])
        here = slice(p * 128, (p + 1) * 128)
        send_a[:, here], send_b[:, here] = to_partners(even, high, low)


def coarse_kernel(
    slabs, narrow, place, skeleton2, inner2, got_a, got_b, plane_a, plane_b, sort,
    solve_h, solve_l, update_h, update_l,
    solved, rest, send_a, send_b,
    parts, vector, product, out_rows,
):
    above, below = from_partners(place[1], narrow, got_a[...], got_b[...])
    plane_above, plane_below = from_partners(place[0], slabs, plane_a[...], plane_b[...])
    half = lanes((48, 128))
    for k in range(4):
        here = slice(k * 128, (k + 1) * 128)
        pack = slice(k // 2 * 128, (k // 2 + 1) * 128)
        up, down = plane_above[:, pack], plane_below[:, pack]
        if k % 2 == 1:
            up, down = roll(up, 64), roll(down, 64)
        value = (
            skeleton2[:, here]
            - inner2[:, here]
            - mid_border(above, below, k * 2)
            - jnp.where(half < 64, down, up)
        )
        top = value.astype(BF16).astype(F32)
        parts[k] = jnp.concatenate([top, value - top], axis=0).astype(BF16)
    arranged = dot(parts[...].reshape(4 * 96, 128), sort[...])
    for child in range(8):
        total = None
        for k in range(4):
            from_columns = slice(child // 4 * 128, (child // 4 + 1) * 128)
            value = (
                arranged[k * 96 : k * 96 + 48, from_columns]
                + arranged[k * 96 + 48 : k * 96 + 96, from_columns]
            )
            moved = roll(value, 32 * (k - child % 4))
            total = moved if total is None else jnp.where(half // 32 == k, moved, total)
        vector[child * 48 : (child + 1) * 48, :] = total
    result = dot3(solve_h[...], solve_l[...], vector[96:, :])
    solution_vector = result[:288]
    for k in range(4):
        out_rows[pl.ds(k, 288, stride=4), :] = roll(solution_vector, -32 * k)
    sol_h, sol_l = halves(solution_vector)
    both = dot(update_h[...], jnp.concatenate([sol_h, sol_l], axis=1))
    product[...] = both[:, :128] + both[:, 128:] + dot(update_l[...], sol_h)
    solved[...] = out_rows[...].T[8:24, :]

    l = lanes((96, 128)) % 4
    sums = []
    for dx in range(3):
        total = None
        for dz in range(3):
            column = None
            for dy in range(3):
                base = (dx * 9 + dy * 3 + dz) * 96
                moved = roll(product[base : base + 96, :], -((dy - 1) * 4 + dz - 1))
                column = moved if column is None else column + moved
            if dz == 0:
                column = jnp.where(l > 0, column, 0.0)
            if dz == 2:
                column = jnp.where(l < 3, column, 0.0)
            total = column if total is None else total + column
        sums.append(total)
    rest[...] = vector[:96, :] - result[288:] - sums[1]
    send_a[...], send_b[...] = to_partners(place[0] % 2 == 0, sums[0], sums[2])


def coarse_edge_kernel(slabs, place, rest, plane_a, plane_b, out, rows):
    above, below = from_partners(place[0], slabs, plane_a[...], plane_b[...])
    value = rest[...] - above - below
    for k in range(4):
        rows[pl.ds(k, 96, stride=4), :] = roll(value, -32 * k)
    out[...] = rows[...].T[4:28, :]


def pair_kernel(place, own, other, out):
    even = place[1] % 2 == 0
    first = jnp.where(even, own[...], other[...])
    second = jnp.where(even, other[...], own[...])
    out[...] = jnp.zeros_like(out)
    out[0:24, :] = first
    out[16:40, :] = out[16:40, :] + second


def gather_kernel(pairs, place, *refs):
    blocks, out, rows = refs[:pairs], refs[pairs], refs[pairs + 1]
    mine = place[1] // 2
    rows[...] = jnp.zeros_like(rows)
    for distance in range(pairs):
        base = pl.multiple_of((mine ^ distance) * 32, 8)
        rows[pl.ds(base, 40), :] = rows[pl.ds(base, 40), :] + blocks[distance][...]
    out[...] = rows[4 : 4 + pairs * 32, :]


def call(kernel, place, operands, outs, scratch=(), flops=0):
    vmem = pl.BlockSpec(memory_space=pltpu.VMEM)
    smem = pl.BlockSpec(memory_space=pltpu.SMEM)
    out_shape = [jax.ShapeDtypeStruct(shape, dtype) for shape, dtype in outs]
    moved = sum(x.size * x.dtype.itemsize for x in list(operands) + out_shape)
    given = ([] if place is None else [place]) + list(operands)
    specs = ([] if place is None else [smem]) + [vmem] * len(operands)
    return pl.pallas_call(
        kernel,
        out_shape=out_shape,
        in_specs=specs,
        out_specs=[vmem] * len(outs),
        scratch_shapes=[pltpu.VMEM(shape, dtype) for shape, dtype in scratch],
        compiler_params=pltpu.CompilerParams(vmem_limit_bytes=VMEM_LIMIT),
        cost_estimate=pl.CostEstimate(flops=flops, bytes_accessed=moved, transcendentals=0),
    )(*given)


def swap(first, second, axis):
    count = lax.axis_size(axis)
    results = []
    for parity, value in enumerate((first, second)):
        pairs = []
        for i in range(parity, count, 2):
            other = (i + 1) % count
            pairs += [(i, other), (other, i)]
        results.append(lax.ppermute(value, axis, pairs))
    return results


def local(rhs, skel1, elim1, update1, skel2, elim2, update2, skel3, elim3, update3):
    slabs, narrow = lax.axis_size("slab"), lax.axis_size("narrow")
    place = jnp.stack([lax.axis_index("slab"), lax.axis_index("narrow")]).astype(jnp.int32)

    solved1, skeleton, inner, edge, send_a, send_b = call(
        fine_kernel,
        place,
        [rhs.reshape(1024, 256), skel1, elim1, update1.reshape(648, 40)],
        [
            ((1024, 160), F32),
            ((4, 24, 1024), F32),
            ((4, 24, 1024), F32),
            ((2, 24, 1024), F32),
            ((24, 384), F32),
            ((24, 384), F32),
        ],
        [
            ((64, 128), F32),
            ((216, 384), F32),
            ((2, 256, 128), F32),
            ((4, 4, 128, 256), BF16),
            ((2, 160, 128), F32),
        ],
        flops=1 << 30,
    )
    got_a, got_b = swap(send_a, send_b, "narrow")
    operators = call(
        operators_kernel,
        None,
        [skel2, elim2, update2.reshape(1296, 144), skel3, elim3, update3.reshape(2592, 288)],
        [((192, 144), BF16)] * 2
        + [((1296, 144), BF16)] * 2
        + [((384, 288), BF16)] * 2
        + [((2592, 288), BF16)] * 2
        + [((256, 256), BF16), ((128, 256), BF16)],
    )
    solve2, update2, solve3, update3 = [operators[2 * i : 2 * i + 2] for i in range(4)]
    sort2, sort3 = operators[8:]

    plane_a, plane_b = swap(
        *call(
            functools.partial(fine_edge_kernel, narrow),
            place,
            [edge, got_a, got_b],
            [((24, 1024), F32)] * 2,
        ),
        "slab",
    )
    solved2, skeleton, inner, edge, send_a, send_b = call(
        functools.partial(mid_kernel, slabs, narrow),
        place,
        [skeleton, inner, got_a, got_b, plane_a, plane_b, sort2, *solve2, *update2],
        [
            ((128, 576), F32),
            ((48, 512), F32),
            ((48, 512), F32),
            ((48, 512), F32),
            ((48, 128), F32),
            ((48, 128), F32),
        ],
        [((16, 48, 256), BF16), ((192, 512), F32), ((1296, 512), F32), ((576, 128), F32)],
        flops=1 << 30,
    )
    got_a, got_b = swap(send_a, send_b, "narrow")
    plane_a, plane_b = swap(
        *call(
            functools.partial(mid_edge_kernel, narrow),
            place,
            [edge, got_a, got_b],
            [((48, 256), F32)] * 2,
        ),
        "slab",
    )
    solved3, rest, send_a, send_b = call(
        functools.partial(coarse_kernel, slabs, narrow),
        place,
        [skeleton, inner, got_a, got_b, plane_a, plane_b, sort3, *solve3, *update3],
        [((16, 1152), F32), ((96, 128), F32), ((96, 128), F32), ((96, 128), F32)],
        [((4, 96, 128), BF16), ((384, 128), F32), ((2592, 128), F32), ((1152, 128), F32)],
        flops=1 << 30,
    )
    plane_a, plane_b = swap(send_a, send_b, "slab")
    (mine,) = call(
        functools.partial(coarse_edge_kernel, slabs),
        place,
        [rest, plane_a, plane_b],
        [((24, 384), F32)],
        [((384, 128), F32)],
    )
    other = lax.ppermute(mine, "narrow", [(i, i ^ 1) for i in range(narrow)])
    (pair,) = call(pair_kernel, place, [mine, other], [((40, 384), F32)])
    pairs = narrow // 2
    blocks = [pair] + [
        lax.ppermute(pair, "narrow", [(i, i ^ (2 * d)) for i in range(narrow)])
        for d in range(1, pairs)
    ]
    (coarse,) = call(
        functools.partial(gather_kernel, pairs),
        place,
        blocks,
        [((pairs * 32, 384), F32)],
        [((pairs * 32 + 8, 384), F32)],
    )
    return (
        solved1.reshape(4, 16, 16, 160),
        solved2.reshape(2, 8, 8, 576),
        solved3.reshape(1, 4, 4, 1152),
        coarse.reshape(1, pairs * 8, 4, 384),
    )


def solution(mesh):
    return jax.shard_map(
        local,
        mesh=mesh,
        in_specs=(P("slab", "narrow", None, None), P(), P(), P(), P(), P(), P(), P(), P(), P()),
        out_specs=(
            P("slab", "narrow", None, None),
            P("slab", "narrow", None, None),
            P("slab", "narrow", None, None),
            P("slab", None, None, None),
        ),
        check_vma=False,
    )
```

```python
import functools

import jax
import jax.numpy as jnp
from jax import lax
from jax.experimental import pallas as pl
from jax.experimental.pallas import tpu as pltpu
from jax.sharding import PartitionSpec as P

F32 = jnp.float32
BF16 = jnp.bfloat16
VMEM_LIMIT = 48 * 1024 * 1024


def dot(a, b):
    return lax.dot_general(a, b, (((1,), (0,)), ((), ())), preferred_element_type=F32)


def halves(x):
    high = x.astype(BF16)
    return high, (x - high.astype(F32)).astype(BF16)


def dot3(a_high, a_low, b):
    b_high, b_low = halves(b)
    return dot(a_high, b_high) + dot(a_low, b_high) + dot(a_high, b_low)


def lanes(shape):
    return lax.broadcasted_iota(jnp.int32, shape, len(shape) - 1)


def roll(x, shift):
    size = x.shape[1]
    shift = shift % size
    return x if shift == 0 else pltpu.roll(x, shift, 1)


def stacked(x):
    high = x.astype(BF16).astype(F32)
    zeros = jnp.zeros((8, x.shape[1]), F32)
    return jnp.concatenate([high, high, x - high, zeros], axis=0).astype(BF16)


def packed_left(ref, block, x):
    high = x.astype(BF16).astype(F32)
    base = block * 128
    ref[:, base : base + 40] = high
    ref[:, base + 40 : base + 80] = x - high
    ref[:, base + 80 : base + 120] = high


def to_partners(even, upward, downward):
    return jnp.where(even, upward, downward), jnp.where(even, downward, upward)


def from_partners(axis, count, first, second):
    index = lax.axis_index(axis)
    even = index % 2 == 0
    above = jnp.where(even, first, second)
    below = jnp.where(even, second, first)
    zeros = jnp.zeros_like(above)
    return jnp.where(index < count - 1, above, zeros), jnp.where(index > 0, below, zeros)


def fine_solve_kernel(
    rhs, skel, elim, update, solution_out, skeleton, cat, packed, send_a, send_b,
    planes, skel_in, elim_in, update_in, left_c, left_u, turned, sems,
):
    copies = [
        pltpu.make_async_copy(elim, elim_in, sems.at[0]),
        pltpu.make_async_copy(skel, skel_in, sems.at[1]),
    ]
    for x in range(4):
        here = pl.ds(x * 256, 256)
        copies.append(pltpu.make_async_copy(rhs.at[here], planes.at[here], sems.at[2 + x]))
    copies.append(pltpu.make_async_copy(update, update_in, sems.at[6]))
    for copy in copies:
        copy.start()
    left_c[...] = jnp.zeros_like(left_c)
    left_u[...] = jnp.zeros_like(left_u)
    copies[0].wait()
    copies[1].wait()
    packed_left(left_c, 0, jnp.concatenate([elim_in[...], skel_in[...]], axis=0))
    solve = left_c[...].astype(BF16)
    half = lanes((40, 128))
    ends = [[jnp.zeros((40, 128), F32)] * 3 for _ in range(2)]
    for x in range(4):
        copies[2 + x].wait()
        for part in range(2):
            turned[part] = planes[x * 256 + part * 128 : x * 256 + (part + 1) * 128, :].T
        for k in range(4):
            vector = jnp.concatenate(
                [turned[part, pl.ds(k, 64, stride=4), :] for part in range(2)], axis=1
            )
            product = dot(solve, stacked(vector[24:64]))
            skeleton[x, :, k * 256 : (k + 1) * 256] = vector[:24] - product[40:64]
            solution_vector = product[:40]
            solution_out[k, x] = solution_vector
            cat[k, x] = stacked(solution_vector)
            q, u = divmod(k * 6 + x, 8)
            first = roll(solution_vector[:, :128], 16 * u)
            last = roll(solution_vector[:, 128:], 16 * u + 16)
            ends[0][q] = jnp.where(half // 16 == u, first, ends[0][q])
            ends[1][q] = jnp.where(half // 16 == u, last, ends[1][q])
    copies[6].wait()
    for dx in range(3):
        packed_left(left_u, dx, update_in[dx * 216 : (dx + 1) * 216, :])
    operator = left_u[...].astype(BF16)
    packed[...] = operator
    z = lanes((24, 384)) % 16
    messages = []
    for end, base in ((0, 144), (1, 0)):
        boundary = jnp.concatenate(ends[end], axis=1)
        right = jnp.concatenate([stacked(roll(boundary, 16 * (2 - d))) for d in range(3)], axis=0)
        messages.append(along_z(dot(operator[base : base + 72], right), 24, z, 15))
    send_a[...], send_b[...] = to_partners(lax.axis_index("narrow") % 2 == 0, messages[1], messages[0])


def along_z(product, rows, z, last):
    minus, zero, plus = [product[d * rows : (d + 1) * rows] for d in range(3)]
    return (
        zero
        + jnp.where(z > 0, roll(minus, 1), 0.0)
        + jnp.where(z < last, roll(plus, -1), 0.0)
    )


def fine_plane(operator, cat, k, c):
    first = max(0, c - 2)
    last = min(3, c)
    columns = operator[:, (first - c + 2) * 128 : (last - c + 3) * 128]
    right = cat[k, first : last + 1].reshape((last + 1 - first) * 128, 256)
    product = dot(columns, right)
    lane = lanes((24, 256))
    sums = [along_z(product[dy * 72 : (dy + 1) * 72], 24, lane % 16, 15) for dy in range(3)]
    return (
        sums[1]
        + jnp.where(lane >= 16, roll(sums[0], 16), 0.0)
        + jnp.where(lane < 240, roll(sums[2], -16), 0.0)
    )


def fine_outside_kernel(cat, packed, edge):
    operator = packed[...]
    for k in range(4):
        for side, c in ((0, 0), (1, 5)):
            edge[side, :, k * 256 : (k + 1) * 256] = fine_plane(operator, cat, k, c)


def fine_inside_kernel(cat, packed, solution_in, after, skeleton, solved, rest, out_rows):
    operator = packed[...]
    for k in range(4):
        for x in range(4):
            here = slice(k * 256, (k + 1) * 256)
            rest[x, :, here] = skeleton[x, :, here] - fine_plane(operator, cat, k, x + 1)
    for x in range(4):
        for part in range(2):
            for k in range(4):
                out_rows[part, pl.ds(k, 40, stride=4), :] = solution_in[
                    k, x, :, part * 128 : (part + 1) * 128
                ]
            solved[x * 256 + part * 128 : x * 256 + (part + 1) * 128, :] = out_rows[part].T


def fine_border(above, below, slot):
    half = lanes((24, 128))
    q, u = divmod(slot, 8)
    here = slice(q * 128, (q + 1) * 128)
    start = jnp.where(half < 16, roll(below[:, here], -16 * u), 0.0)
    end = jnp.where(half >= 112, roll(above[:, here], -16 * u - 16), 0.0)
    return start, end


def fine_edge_kernel(narrow, edge, got_a, got_b, send_a, send_b):
    above, below = from_partners("narrow", narrow, got_a[...], got_b[...])
    even = lax.axis_index("slab") % 2 == 0
    for k in range(4):
        planes = []
        for side, c in ((0, 0), (1, 5)):
            start, end = fine_border(above, below, k * 6 + c)
            planes.append(
                (
                    edge[side, :, k * 256 : k * 256 + 128] + start,
                    edge[side, :, k * 256 + 128 : (k + 1) * 256] + end,
                )
            )
        for part in range(2):
            here = slice(k * 256 + part * 128, k * 256 + (part + 1) * 128)
            send_a[:, here], send_b[:, here] = to_partners(even, planes[1][part], planes[0][part])


def operators_mid_kernel(after, skel, elim, update, solve_h, solve_l, update_h, update_l, sort):
    solve_h[...], solve_l[...] = halves(jnp.concatenate([elim[...], skel[...]], axis=0))
    update_h[...], update_l[...] = halves(update[...])
    row = lax.broadcasted_iota(jnp.int32, (256, 256), 0)
    y, z = row // 16, row % 16
    goal = ((y % 2) * 2 + z % 2) * 64 + (y // 2) * 8 + z // 2
    sort[...] = jnp.where(goal == lanes((256, 256)), 1.0, 0.0).astype(BF16)


def operators_coarse_kernel(after, skel, elim, update, solve_h, solve_l, update_h, update_l, sort):
    solve_h[...], solve_l[...] = halves(jnp.concatenate([elim[...], skel[...]], axis=0))
    update_h[...], update_l[...] = halves(update[...])
    row = lax.broadcasted_iota(jnp.int32, (128, 256), 0)
    x, y, z = row // 64, row // 8 % 8, row % 8
    goal = ((x * 2 + y % 2) * 2 + z % 2) * 32 + (y // 2 + 2) * 4 + z // 2
    sort[...] = jnp.where(goal == lanes((128, 256)), 1.0, 0.0).astype(BF16)


def mid_solve_kernel(
    slabs, narrow, rest1, got_a, got_b, plane_a, plane_b, sort, solve_h, solve_l, update_h, update_l,
    solution_out, skeleton, send_a, send_b,
    parts, vector,
):
    above, below = from_partners("narrow", narrow, got_a[...], got_b[...])
    plane_above, plane_below = from_partners("slab", slabs, plane_a[...], plane_b[...])
    for k in range(4):
        for x in range(4):
            start, end = fine_border(above, below, k * 6 + x + 1)
            here = slice(k * 256, (k + 1) * 256)
            value = rest1[x, :, here] - jnp.concatenate([start, end], axis=1)
            if x == 0:
                value = value - plane_below[:, here]
            if x == 3:
                value = value - plane_above[:, here]
            top = value.astype(BF16).astype(F32)
            parts[k * 4 + x] = jnp.concatenate([top, value - top], axis=0).astype(BF16)
    arranged = dot(parts[...].reshape(16 * 48, 256), sort[...])
    half = lanes((24, 128))
    for k in range(4):
        for dx in range(2):
            pair = []
            for x in (dx, 2 + dx):
                base = (k * 4 + x) * 48
                pair.append(arranged[base : base + 24] + arranged[base + 24 : base + 48])
            for dy in range(2):
                first, second = [v[:, dy * 128 : (dy + 1) * 128] for v in pair]
                here = slice(k * 128, (k + 1) * 128)
                child = (dx * 2 + dy) * 2
                vector[child * 24 : child * 24 + 24, here] = jnp.where(
                    half < 64, first, roll(second, 64)
                )
                vector[child * 24 + 24 : child * 24 + 48, here] = jnp.where(
                    half < 64, roll(first, 64), second
                )
    result = dot3(solve_h[...], solve_l[...], vector[48:, :])
    solution_vector = result[:144]
    solution_out[...] = solution_vector
    skeleton[...] = vector[:48, :] - result[144:]

    j = lanes((144, 128)) // 8 % 8
    ends = []
    for end, wanted in enumerate((0, 7)):
        total = None
        for k in range(4):
            block = solution_vector[:, k * 128 : (k + 1) * 128]
            for x in range(2):
                u = k * 2 + x
                moved = roll(block, 8 * (u - wanted) - 64 * x + 64 * end)
                total = moved if total is None else jnp.where(j == u, moved, total)
        ends.append(total)
    spot = lanes((48, 128))
    l = spot % 8
    right = jnp.where(lanes((144, 128)) < 64, ends[0], ends[1])
    sums = [[], []]
    for dx in range(3):
        rows = []
        for dy in (2, 0):
            base = (dx * 9 + dy * 3) * 48
            rows.append(slice(base, base + 144))
        both = [dot3(update_h[r, :], update_l[r, :], right) for r in rows]
        for end in range(2):
            sums[end].append(along_z(both[end], 48, l, 7))
    x = spot // 8 % 2
    messages = []
    for end in range(2):
        minus, zero, plus = sums[end]
        inside = zero + jnp.where(x == 0, roll(plus, -8), roll(minus, 8))
        outside = jnp.where(x == 0, plus, minus)
        if end == 0:
            messages.append(jnp.where(spot < 64, inside, roll(outside, 64)))
        else:
            messages.append(jnp.where(spot < 64, roll(inside, 64), outside))
    send_a[...], send_b[...] = to_partners(lax.axis_index("narrow") % 2 == 0, messages[1], messages[0])


def mid_update_kernel(solution_in, skeleton, update_h, update_l, rest, edge, product):
    product[...] = dot3(update_h[...], update_l[...], solution_in[...])
    lane = lanes((48, 128))
    i, j, l = lane // 64, lane // 8 % 8, lane % 8
    for k in range(4):
        here = slice(k * 128, (k + 1) * 128)
        totals = []
        for dx in range(3):
            sums = []
            for dy in range(3):
                base = (dx * 9 + dy * 3) * 48
                sums.append(along_z(product[base : base + 144, here], 48, l, 7))
            totals.append(
                sums[1]
                + jnp.where(j > 0, roll(sums[0], 8), 0.0)
                + jnp.where(j < 7, roll(sums[2], -8), 0.0)
            )
        minus, zero, plus = totals
        inside = zero + jnp.where(i == 0, roll(plus, 64), roll(minus, 64))
        rest[:, here] = skeleton[:, here] - inside
        edge[:, here] = jnp.where(i == 0, plus, minus)


def mid_border(above, below, k, a):
    lane = lanes((48, 128))
    j = lane // 8 % 8
    total = jnp.zeros((48, 128), F32)
    for x in range(2):
        start = a * 64 + (k * 2 + x) * 8
        here = lane // 64 == x
        total = jnp.where(here & (j == 0), roll(below, x * 64 - start), total)
        total = jnp.where(here & (j == 7), roll(above, x * 64 + 56 - start), total)
    return total


def mid_edge_kernel(narrow, edge, got_a, got_b, send_a, send_b):
    above, below = from_partners("narrow", narrow, got_a[...], got_b[...])
    even = lax.axis_index("slab") % 2 == 0
    half = lanes((48, 128))
    for p in range(2):
        pair = []
        for k in (2 * p, 2 * p + 1):
            pair.append(edge[:, k * 128 : (k + 1) * 128] + mid_border(above, below, k, 1))
        moved = roll(pair[0], 64)
        low = jnp.where(half >= 64, moved, pair[1])
        high = jnp.where(half < 64, moved, pair[1])
        here = slice(p * 128, (p + 1) * 128)
        send_a[:, here], send_b[:, here] = to_partners(even, high, low)


def mid_solved_kernel(after, solution_in, solved, out_rows):
    for k in range(4):
        out_rows[pl.ds(k, 144, stride=4), :] = solution_in[:, k * 128 : (k + 1) * 128]
    solved[...] = out_rows[...].T


def coarse_solve_kernel(
    slabs, narrow, rest2, got_a, got_b, plane_a, plane_b, sort, solve_h, solve_l, update_h, update_l,
    solution_out, skeleton, send_a, send_b,
    parts, vector,
):
    above, below = from_partners("narrow", narrow, got_a[...], got_b[...])
    plane_above, plane_below = from_partners("slab", slabs, plane_a[...], plane_b[...])
    half = lanes((48, 128))
    for k in range(4):
        here = slice(k * 128, (k + 1) * 128)
        pack = slice(k // 2 * 128, (k // 2 + 1) * 128)
        up, down = plane_above[:, pack], plane_below[:, pack]
        if k % 2 == 1:
            up, down = roll(up, 64), roll(down, 64)
        value = rest2[:, here] - mid_border(above, below, k, 0) - jnp.where(half < 64, down, up)
        top = value.astype(BF16).astype(F32)
        parts[k] = jnp.concatenate([top, value - top], axis=0).astype(BF16)
    arranged = dot(parts[...].reshape(4 * 96, 128), sort[...])
    for child in range(8):
        total = None
        for k in range(4):
            from_columns = slice(child // 4 * 128, (child // 4 + 1) * 128)
            value = (
                arranged[k * 96 : k * 96 + 48, from_columns]
                + arranged[k * 96 + 48 : k * 96 + 96, from_columns]
            )
            moved = roll(value, 32 * (k - child % 4))
            total = moved if total is None else jnp.where(half // 32 == k, moved, total)
        vector[child * 48 : (child + 1) * 48, :] = total
    result = dot3(solve_h[...], solve_l[...], vector[96:, :])
    solution_vector = result[:288]
    solution_out[...] = solution_vector
    skeleton[...] = vector[:96, :] - result[288:]
    low = coarse_plane(update_h, update_l, solution_vector, 2)
    high = coarse_plane(update_h, update_l, solution_vector, 0)
    send_a[...], send_b[...] = to_partners(lax.axis_index("slab") % 2 == 0, high, low)


def coarse_plane(update_h, update_l, solution_vector, dx):
    sol_h, sol_l = halves(solution_vector)
    rows = slice(dx * 864, (dx + 1) * 864)
    both = dot(update_h[rows, :], jnp.concatenate([sol_h, sol_l], axis=1))
    product = both[:, :128] + both[:, 128:] + dot(update_l[rows, :], sol_h)
    l = lanes((96, 128)) % 4
    total = None
    for dz in range(3):
        column = None
        for dy in range(3):
            base = (dy * 3 + dz) * 96
            moved = roll(product[base : base + 96, :], -((dy - 1) * 4 + dz - 1))
            column = moved if column is None else column + moved
        if dz == 0:
            column = jnp.where(l > 0, column, 0.0)
        if dz == 2:
            column = jnp.where(l < 3, column, 0.0)
        total = column if total is None else total + column
    return total


def coarse_update_kernel(after, solution_in, skeleton, update_h, update_l, solved, rest, out_rows):
    solution_vector = solution_in[...]
    rest[...] = skeleton[...] - coarse_plane(update_h, update_l, solution_vector, 1)
    for k in range(4):
        out_rows[pl.ds(k, 288, stride=4), :] = roll(solution_vector, -32 * k)
    columns = out_rows[...].T
    for y in range(4):
        solved[y] = columns[8 + y * 4 : 12 + y * 4, :]


def coarse_edge_kernel(slabs, rest, plane_a, plane_b, out, rows):
    above, below = from_partners("slab", slabs, plane_a[...], plane_b[...])
    value = rest[...] - above - below
    for k in range(4):
        rows[pl.ds(k, 96, stride=4), :] = roll(value, -32 * k)
    out[...] = rows[...].T[4:28, :]


def pair_kernel(own, other, out):
    even = lax.axis_index("narrow") % 2 == 0
    first = jnp.where(even, own[...], other[...])
    second = jnp.where(even, other[...], own[...])
    out[0:16, :] = first[0:16]
    out[16:24, :] = first[16:24] + second[0:8]
    out[24:40, :] = second[8:24]


def gather_kernel(pairs, *refs):
    blocks, out, rows = refs[:pairs], refs[pairs], refs[pairs + 1]
    mine = lax.axis_index("narrow") // 2
    rows[...] = jnp.zeros_like(rows)
    for distance in range(pairs):
        base = pl.multiple_of((mine ^ distance) * 32, 8)
        rows[pl.ds(base, 40), :] = rows[pl.ds(base, 40), :] + blocks[distance][...]
    for y in range(pairs * 8):
        out[y] = rows[4 + y * 4 : 8 + y * 4, :]


def call(kernel, operands, outs, scratch=(), flops=0, unread=(), where=pltpu.VMEM, sems=0):
    vmem = pl.BlockSpec(memory_space=pltpu.VMEM)
    out_shape = [jax.ShapeDtypeStruct(shape, dtype) for shape, dtype in outs]
    moved = sum(
        x.size * x.dtype.itemsize
        for x in [v for i, v in enumerate(operands) if i not in unread] + out_shape
    )
    specs = [
        pl.BlockSpec(memory_space=pl.ANY if i in unread else where) for i in range(len(operands))
    ]
    scratch_shapes = [pltpu.VMEM(shape, dtype) for shape, dtype in scratch]
    if sems:
        scratch_shapes.append(pltpu.SemaphoreType.DMA((sems,)))
    return pl.pallas_call(
        kernel,
        out_shape=out_shape,
        in_specs=specs,
        out_specs=[vmem] * len(outs),
        scratch_shapes=scratch_shapes,
        compiler_params=pltpu.CompilerParams(vmem_limit_bytes=VMEM_LIMIT),
        cost_estimate=pl.CostEstimate(flops=flops, bytes_accessed=moved, transcendentals=0),
    )(*operands)


def swap(first, second, axis):
    count = lax.axis_size(axis)
    results = []
    for parity, value in enumerate((first, second)):
        pairs = []
        for i in range(parity, count, 2):
            other = (i + 1) % count
            pairs += [(i, other), (other, i)]
        results.append(lax.ppermute(value, axis, pairs))
    return results


def local(rhs, skel1, elim1, update1, skel2, elim2, update2, skel3, elim3, update3):
    slabs, narrow = lax.axis_size("slab"), lax.axis_size("narrow")

    solution1, skeleton, cat, packed, send_a, send_b = call(
        fine_solve_kernel,
        [rhs.reshape(1024, 256), skel1, elim1, update1.reshape(648, 40)],
        [
            ((4, 4, 40, 256), F32),
            ((4, 24, 1024), F32),
            ((4, 4, 128, 256), BF16),
            ((216, 384), BF16),
            ((24, 384), F32),
            ((24, 384), F32),
        ],
        [
            ((1024, 256), F32),
            ((24, 40), F32),
            ((40, 40), F32),
            ((648, 40), F32),
            ((64, 128), F32),
            ((216, 384), F32),
            ((2, 256, 128), F32),
        ],
        flops=1 << 29,
        where=pltpu.HBM,
        sems=7,
    )
    got_a, got_b = swap(send_a, send_b, "narrow")
    (edge,) = call(fine_outside_kernel, [cat, packed], [((2, 24, 1024), F32)], flops=1 << 30)
    send_a, send_b = call(
        functools.partial(fine_edge_kernel, narrow),
        [edge, got_a, got_b],
        [((24, 1024), F32)] * 2,
    )
    plane_a, plane_b = swap(send_a, send_b, "slab")
    solved1, rest = call(
        fine_inside_kernel,
        [cat, packed, solution1, send_a, skeleton],
        [((1024, 160), F32), ((4, 24, 1024), F32)],
        [((2, 160, 128), F32)],
        flops=1 << 30,
        unread=(3,),
    )
    *solve2, update2_h, update2_l, sort2 = call(
        operators_mid_kernel,
        [send_a, skel2, elim2, update2.reshape(1296, 144)],
        [((192, 144), BF16)] * 2 + [((1296, 144), BF16)] * 2 + [((256, 256), BF16)],
        unread=(0,),
    )

    solution2, skeleton, send_a, send_b = call(
        functools.partial(mid_solve_kernel, slabs, narrow),
        [rest, got_a, got_b, plane_a, plane_b, sort2, *solve2, update2_h, update2_l],
        [((144, 512), F32), ((48, 512), F32), ((48, 128), F32), ((48, 128), F32)],
        [((16, 48, 256), BF16), ((192, 512), F32)],
        flops=1 << 29,
    )
    got_a, got_b = swap(send_a, send_b, "narrow")
    rest, edge = call(
        mid_update_kernel,
        [solution2, skeleton, update2_h, update2_l],
        [((48, 512), F32), ((48, 512), F32)],
        [((1296, 512), F32)],
        flops=1 << 30,
    )
    send_a, send_b = call(
        functools.partial(mid_edge_kernel, narrow),
        [edge, got_a, got_b],
        [((48, 256), F32)] * 2,
    )
    plane_a, plane_b = swap(send_a, send_b, "slab")
    (solved2,) = call(
        mid_solved_kernel,
        [send_a, solution2],
        [((128, 576), F32)],
        [((576, 128), F32)],
        unread=(0,),
    )
    *solve3, update3_h, update3_l, sort3 = call(
        operators_coarse_kernel,
        [send_a, skel3, elim3, update3.reshape(2592, 288)],
        [((384, 288), BF16)] * 2 + [((2592, 288), BF16)] * 2 + [((128, 256), BF16)],
        unread=(0,),
    )

    solution3, skeleton, send_a, send_b = call(
        functools.partial(coarse_solve_kernel, slabs, narrow),
        [rest, got_a, got_b, plane_a, plane_b, sort3, *solve3, update3_h, update3_l],
        [((288, 128), F32), ((96, 128), F32), ((96, 128), F32), ((96, 128), F32)],
        [((4, 96, 128), BF16), ((384, 128), F32)],
        flops=1 << 29,
    )
    plane_a, plane_b = swap(send_a, send_b, "slab")
    solved3, rest = call(
        coarse_update_kernel,
        [send_a, solution3, skeleton, update3_h, update3_l],
        [((4, 4, 1152), F32), ((96, 128), F32)],
        [((1152, 128), F32)],
        flops=1 << 29,
        unread=(0,),
    )
    (mine,) = call(
        functools.partial(coarse_edge_kernel, slabs),
        [rest, plane_a, plane_b],
        [((24, 384), F32)],
        [((384, 128), F32)],
    )
    other = lax.ppermute(mine, "narrow", [(i, i ^ 1) for i in range(narrow)])
    (pair,) = call(pair_kernel, [mine, other], [((40, 384), F32)])
    pairs = narrow // 2
    blocks = [pair] + [
        lax.ppermute(pair, "narrow", [(i, i ^ (2 * d)) for i in range(narrow)])
        for d in range(1, pairs)
    ]
    (coarse,) = call(
        functools.partial(gather_kernel, pairs),
        blocks,
        [((pairs * 8, 4, 384), F32)],
        [((pairs * 32 + 8, 384), F32)],
    )
    return (
        solved1.reshape(4, 16, 16, 160),
        solved2.reshape(2, 8, 8, 576),
        solved3.reshape(1, 4, 4, 1152),
        coarse.reshape(1, pairs * 8, 4, 384),
    )


def solution(mesh):
    return jax.shard_map(
        local,
        mesh=mesh,
        in_specs=(P("slab", "narrow", None, None), P(), P(), P(), P(), P(), P(), P(), P(), P()),
        out_specs=(
            P("slab", "narrow", None, None),
            P("slab", "narrow", None, None),
            P("slab", "narrow", None, None),
            P("slab", None, None, None),
        ),
        check_vma=False,
    )
```

```python
import functools

import jax
import jax.numpy as jnp
from jax import lax
from jax.experimental import pallas as pl
from jax.experimental.pallas import tpu as pltpu
from jax.sharding import PartitionSpec as P

F32 = jnp.float32
BF16 = jnp.bfloat16
VMEM_LIMIT = 20 * 1024 * 1024


def dot(a, b):
    return lax.dot_general(a, b, (((1,), (0,)), ((), ())), preferred_element_type=F32)


def halves(x):
    high = x.astype(BF16)
    return high, (x - high.astype(F32)).astype(BF16)


def dot3(a_high, a_low, b):
    b_high, b_low = halves(b)
    return dot(a_high, b_high) + dot(a_low, b_high) + dot(a_high, b_low)


def lanes(shape):
    return lax.broadcasted_iota(jnp.int32, shape, len(shape) - 1)


def roll(x, shift):
    size = x.shape[1]
    shift = shift % size
    return x if shift == 0 else pltpu.roll(x, shift, 1)


def stacked(x):
    high = x.astype(BF16).astype(F32)
    zeros = jnp.zeros((8, x.shape[1]), F32)
    return jnp.concatenate([high, high, x - high, zeros], axis=0).astype(BF16)


def packed_left(ref, block, x):
    high = x.astype(BF16).astype(F32)
    base = block * 128
    ref[:, base : base + 40] = high
    ref[:, base + 40 : base + 80] = x - high
    ref[:, base + 80 : base + 120] = high


def to_partners(even, upward, downward):
    return jnp.where(even, upward, downward), jnp.where(even, downward, upward)


def from_partners(axis, count, first, second):
    index = lax.axis_index(axis)
    even = index % 2 == 0
    above = jnp.where(even, first, second)
    below = jnp.where(even, second, first)
    zeros = jnp.zeros_like(above)
    return jnp.where(index < count - 1, above, zeros), jnp.where(index > 0, below, zeros)


def fine_ends_kernel(rhs, send_a, send_b, sems):
    upward = jnp.where(lax.axis_index("narrow") % 2 == 0, 15, 0)
    copies = [
        pltpu.make_async_copy(rhs.at[:, upward], send_a, sems.at[0]),
        pltpu.make_async_copy(rhs.at[:, 15 - upward], send_b, sems.at[1]),
    ]
    for copy in copies:
        copy.start()
    for copy in copies:
        copy.wait()


def fine_solve_kernel(
    rhs, skel, elim, update, solution_out, skeleton, cat, packed, solver,
    planes, skel_in, elim_in, update_in, left_c, left_u, turned, sems,
):
    copies = [
        pltpu.make_async_copy(elim, elim_in, sems.at[0]),
        pltpu.make_async_copy(skel, skel_in, sems.at[1]),
    ]
    for x in range(4):
        here = pl.ds(x * 256, 256)
        copies.append(pltpu.make_async_copy(rhs.at[here], planes.at[here], sems.at[2 + x]))
    copies.append(pltpu.make_async_copy(update, update_in, sems.at[6]))
    for copy in copies:
        copy.start()
    left_c[...] = jnp.zeros_like(left_c)
    left_u[...] = jnp.zeros_like(left_u)
    copies[0].wait()
    copies[1].wait()
    packed_left(left_c, 0, jnp.concatenate([elim_in[...], skel_in[...]], axis=0))
    solve = left_c[...].astype(BF16)
    solver[...] = solve
    for x in range(4):
        copies[2 + x].wait()
        for part in range(2):
            turned[part] = planes[x * 256 + part * 128 : x * 256 + (part + 1) * 128, :].T
        for k in range(4):
            vector = jnp.concatenate(
                [turned[part, pl.ds(k, 64, stride=4), :] for part in range(2)], axis=1
            )
            product = dot(solve, stacked(vector[24:64]))
            skeleton[x, :, k * 256 : (k + 1) * 256] = vector[:24] - product[40:64]
            solution_vector = product[:40]
            solution_out[k, x] = solution_vector
            cat[k, x] = stacked(solution_vector)
    copies[6].wait()
    for dx in range(3):
        packed_left(left_u, dx, update_in[dx * 216 : (dx + 1) * 216, :])
    packed[...] = left_u[...].astype(BF16)


def along_z(product, rows, z, last):
    minus, zero, plus = [product[d * rows : (d + 1) * rows] for d in range(3)]
    return (
        zero
        + jnp.where(z > 0, roll(minus, 1), 0.0)
        + jnp.where(z < last, roll(plus, -1), 0.0)
    )


def fine_plane(operator, cat, k, c):
    first = max(0, c - 2)
    last = min(3, c)
    columns = operator[:, (first - c + 2) * 128 : (last - c + 3) * 128]
    right = cat[k, first : last + 1].reshape((last + 1 - first) * 128, 256)
    product = dot(columns, right)
    lane = lanes((24, 256))
    sums = [along_z(product[dy * 72 : (dy + 1) * 72], 24, lane % 16, 15) for dy in range(3)]
    return (
        sums[1]
        + jnp.where(lane >= 16, roll(sums[0], 16), 0.0)
        + jnp.where(lane < 240, roll(sums[2], -16), 0.0)
    )


def fine_outside_kernel(cat, packed, edge):
    operator = packed[...]
    for k in range(4):
        for side, c in ((0, 0), (1, 5)):
            edge[side, :, k * 256 : (k + 1) * 256] = fine_plane(operator, cat, k, c)


def fine_inside_kernel(cat, packed, solution_in, after, skeleton, solved, rest, out_rows):
    operator = packed[...]
    for k in range(4):
        for x in range(4):
            here = slice(k * 256, (k + 1) * 256)
            rest[x, :, here] = skeleton[x, :, here] - fine_plane(operator, cat, k, x + 1)
    for x in range(4):
        for part in range(2):
            for k in range(4):
                out_rows[part, pl.ds(k, 40, stride=4), :] = solution_in[
                    k, x, :, part * 128 : (part + 1) * 128
                ]
            solved[x * 256 + part * 128 : x * 256 + (part + 1) * 128, :] = out_rows[part].T


def fine_border(above, below, k, c):
    half = lanes((24, 128))
    here = slice(k * 128, (k + 1) * 128)
    start = jnp.where(half < 16, roll(below[:, here], -16 * c), 0.0)
    end = jnp.where(half >= 112, roll(above[:, here], 112 - 16 * c), 0.0)
    return start, end


def fine_edge_kernel(
    narrow, edge, packed, solver, got_a, got_b, sum_above, sum_below, send_a, send_b, turned
):
    above, below = from_partners("narrow", narrow, got_a[...], got_b[...])
    turned[...] = jnp.concatenate([below, above], axis=0).T
    vectors = [turned[pl.ds(k, 64, stride=4), :][24:64] for k in range(4)]
    solution_vector = dot(solver[...], stacked(jnp.concatenate(vectors, axis=1)))[:40]
    operator = packed[...]
    half = lanes((40, 128))
    z = lanes((24, 512)) % 16
    sums = []
    for side, base in ((0, 0), (1, 144)):
        blocks = []
        for k in range(4):
            block = roll(solution_vector[:, k * 128 : (k + 1) * 128], 64 * side)
            blocks.append(jnp.where(half < 64, block, 0.0))
        right = []
        for d in range(3):
            moved = [roll(block, 16 * (2 - d)) for block in blocks]
            right.append(stacked(jnp.concatenate(moved, axis=1)))
        product = dot(operator[base : base + 72], jnp.concatenate(right, axis=0))
        sums.append(along_z(product, 24, z, 15))
    below, above = sums
    sum_below[...] = below
    sum_above[...] = above
    even = lax.axis_index("slab") % 2 == 0
    for k in range(4):
        planes = []
        for side, c in ((0, 0), (1, 5)):
            start, end = fine_border(above, below, k, c)
            planes.append(
                (
                    edge[side, :, k * 256 : k * 256 + 128] + start,
                    edge[side, :, k * 256 + 128 : (k + 1) * 256] + end,
                )
            )
        for part in range(2):
            here = slice(k * 256 + part * 128, k * 256 + (part + 1) * 128)
            send_a[:, here], send_b[:, here] = to_partners(even, planes[1][part], planes[0][part])


def operators_mid_kernel(after, skel, elim, update, solve_h, solve_l, update_h, update_l, sort):
    solve_h[...], solve_l[...] = halves(jnp.concatenate([elim[...], skel[...]], axis=0))
    update_h[...], update_l[...] = halves(update[...])
    row = lax.broadcasted_iota(jnp.int32, (256, 256), 0)
    y, z = row // 16, row % 16
    goal = ((y % 2) * 2 + z % 2) * 64 + (y // 2) * 8 + z // 2
    sort[...] = jnp.where(goal == lanes((256, 256)), 1.0, 0.0).astype(BF16)


def operators_coarse_kernel(after, skel, elim, update, solve_h, solve_l, update_h, update_l, sort):
    solve_h[...], solve_l[...] = halves(jnp.concatenate([elim[...], skel[...]], axis=0))
    update_h[...], update_l[...] = halves(update[...])
    row = lax.broadcasted_iota(jnp.int32, (128, 256), 0)
    x, y, z = row // 64, row // 8 % 8, row % 8
    goal = ((x * 2 + y % 2) * 2 + z % 2) * 32 + (y // 2 + 2) * 4 + z // 2
    sort[...] = jnp.where(goal == lanes((128, 256)), 1.0, 0.0).astype(BF16)


def mid_solve_kernel(
    slabs, rest1, above, below, plane_a, plane_b, sort, solve_h, solve_l, update_h, update_l,
    solution_out, skeleton, send_a, send_b,
    parts, vector,
):
    plane_above, plane_below = from_partners("slab", slabs, plane_a[...], plane_b[...])
    for k in range(4):
        for x in range(4):
            start, end = fine_border(above, below, k, x + 1)
            here = slice(k * 256, (k + 1) * 256)
            value = rest1[x, :, here] - jnp.concatenate([start, end], axis=1)
            if x == 0:
                value = value - plane_below[:, here]
            if x == 3:
                value = value - plane_above[:, here]
            top = value.astype(BF16).astype(F32)
            parts[k * 4 + x] = jnp.concatenate([top, value - top], axis=0).astype(BF16)
    arranged = dot(parts[...].reshape(16 * 48, 256), sort[...])
    half = lanes((24, 128))
    for k in range(4):
        for dx in range(2):
            pair = []
            for x in (dx, 2 + dx):
                base = (k * 4 + x) * 48
                pair.append(arranged[base : base + 24] + arranged[base + 24 : base + 48])
            for dy in range(2):
                first, second = [v[:, dy * 128 : (dy + 1) * 128] for v in pair]
                here = slice(k * 128, (k + 1) * 128)
                child = (dx * 2 + dy) * 2
                vector[child * 24 : child * 24 + 24, here] = jnp.where(
                    half < 64, first, roll(second, 64)
                )
                vector[child * 24 + 24 : child * 24 + 48, here] = jnp.where(
                    half < 64, roll(first, 64), second
                )
    result = dot3(solve_h[...], solve_l[...], vector[48:, :])
    solution_vector = result[:144]
    solution_out[...] = solution_vector
    skeleton[...] = vector[:48, :] - result[144:]

    j = lanes((144, 128)) // 8 % 8
    ends = []
    for end, wanted in enumerate((0, 7)):
        total = None
        for k in range(4):
            block = solution_vector[:, k * 128 : (k + 1) * 128]
            for x in range(2):
                u = k * 2 + x
                moved = roll(block, 8 * (u - wanted) - 64 * x + 64 * end)
                total = moved if total is None else jnp.where(j == u, moved, total)
        ends.append(total)
    spot = lanes((48, 128))
    l = spot % 8
    right = jnp.where(lanes((144, 128)) < 64, ends[0], ends[1])
    sums = [[], []]
    for dx in range(3):
        rows = []
        for dy in (2, 0):
            base = (dx * 9 + dy * 3) * 48
            rows.append(slice(base, base + 144))
        both = [dot3(update_h[r, :], update_l[r, :], right) for r in rows]
        for end in range(2):
            sums[end].append(along_z(both[end], 48, l, 7))
    x = spot // 8 % 2
    messages = []
    for end in range(2):
        minus, zero, plus = sums[end]
        inside = zero + jnp.where(x == 0, roll(plus, -8), roll(minus, 8))
        outside = jnp.where(x == 0, plus, minus)
        if end == 0:
            messages.append(jnp.where(spot < 64, inside, roll(outside, 64)))
        else:
            messages.append(jnp.where(spot < 64, roll(inside, 64), outside))
    send_a[...], send_b[...] = to_partners(lax.axis_index("narrow") % 2 == 0, messages[1], messages[0])


def mid_update_kernel(solution_in, skeleton, update_h, update_l, rest, edge, product):
    product[...] = dot3(update_h[...], update_l[...], solution_in[...])
    lane = lanes((48, 128))
    i, j, l = lane // 64, lane // 8 % 8, lane % 8
    for k in range(4):
        here = slice(k * 128, (k + 1) * 128)
        totals = []
        for dx in range(3):
            sums = []
            for dy in range(3):
                base = (dx * 9 + dy * 3) * 48
                sums.append(along_z(product[base : base + 144, here], 48, l, 7))
            totals.append(
                sums[1]
                + jnp.where(j > 0, roll(sums[0], 8), 0.0)
                + jnp.where(j < 7, roll(sums[2], -8), 0.0)
            )
        minus, zero, plus = totals
        inside = zero + jnp.where(i == 0, roll(plus, 64), roll(minus, 64))
        rest[:, here] = skeleton[:, here] - inside
        edge[:, here] = jnp.where(i == 0, plus, minus)


def mid_border(above, below, k, a):
    lane = lanes((48, 128))
    j = lane // 8 % 8
    total = jnp.zeros((48, 128), F32)
    for x in range(2):
        start = a * 64 + (k * 2 + x) * 8
        here = lane // 64 == x
        total = jnp.where(here & (j == 0), roll(below, x * 64 - start), total)
        total = jnp.where(here & (j == 7), roll(above, x * 64 + 56 - start), total)
    return total


def mid_edge_kernel(narrow, edge, got_a, got_b, send_a, send_b):
    above, below = from_partners("narrow", narrow, got_a[...], got_b[...])
    even = lax.axis_index("slab") % 2 == 0
    half = lanes((48, 128))
    for p in range(2):
        pair = []
        for k in (2 * p, 2 * p + 1):
            pair.append(edge[:, k * 128 : (k + 1) * 128] + mid_border(above, below, k, 1))
        moved = roll(pair[0], 64)
        low = jnp.where(half >= 64, moved, pair[1])
        high = jnp.where(half < 64, moved, pair[1])
        here = slice(p * 128, (p + 1) * 128)
        send_a[:, here], send_b[:, here] = to_partners(even, high, low)


def mid_solved_kernel(after, solution_in, solved, out_rows):
    for k in range(4):
        out_rows[pl.ds(k, 144, stride=4), :] = solution_in[:, k * 128 : (k + 1) * 128]
    solved[...] = out_rows[...].T


def coarse_solve_kernel(
    slabs, narrow, rest2, got_a, got_b, plane_a, plane_b, sort, solve_h, solve_l, update_h, update_l,
    solution_out, skeleton, send_a, send_b,
    parts, vector,
):
    above, below = from_partners("narrow", narrow, got_a[...], got_b[...])
    plane_above, plane_below = from_partners("slab", slabs, plane_a[...], plane_b[...])
    half = lanes((48, 128))
    for k in range(4):
        here = slice(k * 128, (k + 1) * 128)
        pack = slice(k // 2 * 128, (k // 2 + 1) * 128)
        up, down = plane_above[:, pack], plane_below[:, pack]
        if k % 2 == 1:
            up, down = roll(up, 64), roll(down, 64)
        value = rest2[:, here] - mid_border(above, below, k, 0) - jnp.where(half < 64, down, up)
        top = value.astype(BF16).astype(F32)
        parts[k] = jnp.concatenate([top, value - top], axis=0).astype(BF16)
    arranged = dot(parts[...].reshape(4 * 96, 128), sort[...])
    for child in range(8):
        total = None
        for k in range(4):
            from_columns = slice(child // 4 * 128, (child // 4 + 1) * 128)
            value = (
                arranged[k * 96 : k * 96 + 48, from_columns]
                + arranged[k * 96 + 48 : k * 96 + 96, from_columns]
            )
            moved = roll(value, 32 * (k - child % 4))
            total = moved if total is None else jnp.where(half // 32 == k, moved, total)
        vector[child * 48 : (child + 1) * 48, :] = total
    result = dot3(solve_h[...], solve_l[...], vector[96:, :])
    solution_vector = result[:288]
    solution_out[...] = solution_vector
    skeleton[...] = vector[:96, :] - result[288:]
    low = coarse_plane(update_h, update_l, solution_vector, 2)
    high = coarse_plane(update_h, update_l, solution_vector, 0)
    send_a[...], send_b[...] = to_partners(lax.axis_index("slab") % 2 == 0, high, low)


def coarse_plane(update_h, update_l, solution_vector, dx):
    sol_h, sol_l = halves(solution_vector)
    rows = slice(dx * 864, (dx + 1) * 864)
    both = dot(update_h[rows, :], jnp.concatenate([sol_h, sol_l], axis=1))
    product = both[:, :128] + both[:, 128:] + dot(update_l[rows, :], sol_h)
    l = lanes((96, 128)) % 4
    total = None
    for dz in range(3):
        column = None
        for dy in range(3):
            base = (dy * 3 + dz) * 96
            moved = roll(product[base : base + 96, :], -((dy - 1) * 4 + dz - 1))
            column = moved if column is None else column + moved
        if dz == 0:
            column = jnp.where(l > 0, column, 0.0)
        if dz == 2:
            column = jnp.where(l < 3, column, 0.0)
        total = column if total is None else total + column
    return total


def coarse_update_kernel(after, solution_in, skeleton, update_h, update_l, solved, rest, out_rows):
    solution_vector = solution_in[...]
    rest[...] = skeleton[...] - coarse_plane(update_h, update_l, solution_vector, 1)
    for k in range(4):
        out_rows[pl.ds(k, 288, stride=4), :] = roll(solution_vector, -32 * k)
    columns = out_rows[...].T
    for y in range(4):
        solved[y] = columns[8 + y * 4 : 12 + y * 4, :]


def coarse_edge_kernel(slabs, rest, plane_a, plane_b, out, rows):
    above, below = from_partners("slab", slabs, plane_a[...], plane_b[...])
    value = rest[...] - above - below
    for k in range(4):
        rows[pl.ds(k, 96, stride=4), :] = roll(value, -32 * k)
    out[...] = rows[...].T[4:28, :]


def join_kernel(*refs):
    for i, block in enumerate(refs[:-1]):
        refs[-1][i * 24 : (i + 1) * 24, :] = block[...]


def gather_kernel(chips, own, other, out, rows):
    mine = lax.axis_index("narrow")
    rows[...] = jnp.zeros_like(rows)
    for distance in range(chips):
        for parity, blocks in enumerate((own, other)):
            base = pl.multiple_of((mine ^ (distance * 2 + parity)) * 16, 8)
            here = pl.ds(base, 24)
            rows[here, :] = rows[here, :] + blocks[distance * 24 : (distance + 1) * 24, :]
    for y in range(chips * 8):
        out[y] = rows[4 + y * 4 : 8 + y * 4, :]


def call(kernel, operands, outs, scratch=(), flops=0, unread=(), where=pltpu.VMEM, sems=0):
    vmem = pl.BlockSpec(memory_space=pltpu.VMEM)
    out_shape = [jax.ShapeDtypeStruct(shape, dtype) for shape, dtype in outs]
    moved = sum(
        x.size * x.dtype.itemsize
        for x in [v for i, v in enumerate(operands) if i not in unread] + out_shape
    )
    specs = [
        pl.BlockSpec(memory_space=pl.ANY if i in unread else where) for i in range(len(operands))
    ]
    scratch_shapes = [pltpu.VMEM(shape, dtype) for shape, dtype in scratch]
    if sems:
        scratch_shapes.append(pltpu.SemaphoreType.DMA((sems,)))
    return pl.pallas_call(
        kernel,
        out_shape=out_shape,
        in_specs=specs,
        out_specs=[vmem] * len(outs),
        scratch_shapes=scratch_shapes,
        compiler_params=pltpu.CompilerParams(vmem_limit_bytes=VMEM_LIMIT),
        cost_estimate=pl.CostEstimate(flops=flops, bytes_accessed=moved, transcendentals=0),
    )(*operands)


def swap_narrow(first, second):
    count = lax.axis_size("narrow")
    pairs = [[(i, (i + 1 if i % 2 == parity else i - 1) % count) for i in range(count)] for parity in (0, 1)]
    return [lax.ppermute(value, "narrow", pair) for value, pair in zip((first, second), pairs)]


def swap_slab(first, second):
    slabs, narrow = lax.axis_size("slab"), lax.axis_size("narrow")
    results = []
    for parity, value in enumerate((first, second)):
        pairs = []
        for i in range(slabs):
            j = i + 1 if i % 2 == parity else i - 1
            for n in range(narrow):
                other = j * narrow + n if 0 <= j < slabs else i * narrow + (n ^ 1)
                pairs.append((i * narrow + n, other))
        results.append(lax.ppermute(value, ("slab", "narrow"), pairs))
    return results


def local(rhs, skel1, elim1, update1, skel2, elim2, update2, skel3, elim3, update3):
    slabs, narrow = lax.axis_size("slab"), lax.axis_size("narrow")

    in_hbm = [
        pltpu.with_memory_space_constraint(x, pltpu.HBM)
        for x in (rhs, rhs.reshape(1024, 256), skel1, elim1, update1.reshape(648, 40))
    ]
    got_a, got_b = swap_narrow(
        *call(fine_ends_kernel, in_hbm[:1], [((4, 16, 256), F32)] * 2, where=pltpu.HBM, sems=2)
    )
    solution1, skeleton, cat, packed, solver = call(
        fine_solve_kernel,
        in_hbm[1:],
        [
            ((4, 4, 40, 256), F32),
            ((4, 24, 1024), F32),
            ((4, 4, 128, 256), BF16),
            ((216, 384), BF16),
            ((64, 128), BF16),
        ],
        [
            ((1024, 256), F32),
            ((24, 40), F32),
            ((40, 40), F32),
            ((648, 40), F32),
            ((64, 128), F32),
            ((216, 384), F32),
            ((2, 256, 128), F32),
        ],
        flops=1 << 29,
        where=pltpu.HBM,
        sems=7,
    )
    (edge,) = call(fine_outside_kernel, [cat, packed], [((2, 24, 1024), F32)], flops=1 << 30)
    above, below, send_a, send_b = call(
        functools.partial(fine_edge_kernel, narrow),
        [edge, packed, solver, got_a.reshape(64, 256), got_b.reshape(64, 256)],
        [((24, 512), F32)] * 2 + [((24, 1024), F32)] * 2,
        [((256, 128), F32)],
    )
    after = send_a
    plane_a, plane_b = swap_slab(send_a, send_b)
    solved1, rest = call(
        fine_inside_kernel,
        [cat, packed, solution1, send_a, skeleton],
        [((1024, 160), F32), ((4, 24, 1024), F32)],
        [((2, 160, 128), F32)],
        flops=1 << 30,
        unread=(3,),
    )
    *solve2, update2_h, update2_l, sort2 = call(
        operators_mid_kernel,
        [send_a, skel2, elim2, update2.reshape(1296, 144)],
        [((192, 144), BF16)] * 2 + [((1296, 144), BF16)] * 2 + [((256, 256), BF16)],
        unread=(0,),
    )

    solution2, skeleton, send_a, send_b = call(
        functools.partial(mid_solve_kernel, slabs),
        [rest, above, below, plane_a, plane_b, sort2, *solve2, update2_h, update2_l],
        [((144, 512), F32), ((48, 512), F32), ((48, 128), F32), ((48, 128), F32)],
        [((16, 48, 256), BF16), ((192, 512), F32)],
        flops=1 << 29,
    )
    got_a, got_b = swap_narrow(send_a, send_b)
    rest, edge = call(
        mid_update_kernel,
        [solution2, skeleton, update2_h, update2_l],
        [((48, 512), F32), ((48, 512), F32)],
        [((1296, 512), F32)],
        flops=1 << 30,
    )
    send_a, send_b = call(
        functools.partial(mid_edge_kernel, narrow),
        [edge, got_a, got_b],
        [((48, 256), F32)] * 2,
    )
    plane_a, plane_b = swap_slab(send_a, send_b)
    (solved2,) = call(
        mid_solved_kernel,
        [send_a, solution2],
        [((128, 576), F32)],
        [((576, 128), F32)],
        unread=(0,),
    )
    *solve3, update3_h, update3_l, sort3 = call(
        operators_coarse_kernel,
        [after, skel3, elim3, update3.reshape(2592, 288)],
        [((384, 288), BF16)] * 2 + [((2592, 288), BF16)] * 2 + [((128, 256), BF16)],
        unread=(0,),
    )

    solution3, skeleton, send_a, send_b = call(
        functools.partial(coarse_solve_kernel, slabs, narrow),
        [rest, got_a, got_b, plane_a, plane_b, sort3, *solve3, update3_h, update3_l],
        [((288, 128), F32), ((96, 128), F32), ((96, 128), F32), ((96, 128), F32)],
        [((4, 96, 128), BF16), ((384, 128), F32)],
        flops=1 << 29,
    )
    plane_a, plane_b = swap_slab(send_a, send_b)
    solved3, rest = call(
        coarse_update_kernel,
        [send_a, solution3, skeleton, update3_h, update3_l],
        [((4, 4, 1152), F32), ((96, 128), F32)],
        [((1152, 128), F32)],
        flops=1 << 29,
        unread=(0,),
    )
    (mine,) = call(
        functools.partial(coarse_edge_kernel, slabs),
        [rest, plane_a, plane_b],
        [((24, 384), F32)],
        [((384, 128), F32)],
    )
    chips = narrow // 2
    blocks = [mine] + [
        lax.ppermute(mine, "narrow", [(i, i ^ (2 * d)) for i in range(narrow)])
        for d in range(1, chips)
    ]
    (own,) = call(join_kernel, blocks, [((chips * 24, 384), F32)])
    other = lax.ppermute(own, "narrow", [(i, i ^ 1) for i in range(narrow)])
    (coarse,) = call(
        functools.partial(gather_kernel, chips),
        [own, other],
        [((chips * 8, 4, 384), F32)],
        [((chips * 32 + 8, 384), F32)],
    )
    return (
        solved1.reshape(4, 16, 16, 160),
        solved2.reshape(2, 8, 8, 576),
        solved3.reshape(1, 4, 4, 1152),
        coarse.reshape(1, chips * 8, 4, 384),
    )


def solution(mesh):
    return jax.shard_map(
        local,
        mesh=mesh,
        in_specs=(P("slab", "narrow", None, None), P(), P(), P(), P(), P(), P(), P(), P(), P()),
        out_specs=(
            P("slab", "narrow", None, None),
            P("slab", "narrow", None, None),
            P("slab", "narrow", None, None),
            P("slab", None, None, None),
        ),
        check_vma=False,
    )
```

```python
import functools

import jax
import jax.numpy as jnp
from jax import lax
from jax.experimental import pallas as pl
from jax.experimental.pallas import tpu as pltpu
from jax.sharding import PartitionSpec as P

F32 = jnp.float32
BF16 = jnp.bfloat16
VMEM_LIMIT = 20 * 1024 * 1024


def dot(a, b):
    return lax.dot_general(a, b, (((1,), (0,)), ((), ())), preferred_element_type=F32)


def halves(x):
    high = x.astype(BF16)
    return high, (x - high.astype(F32)).astype(BF16)


def dot3(a_high, a_low, b):
    b_high, b_low = halves(b)
    return dot(a_high, b_high) + dot(a_low, b_high) + dot(a_high, b_low)


def lanes(shape):
    return lax.broadcasted_iota(jnp.int32, shape, len(shape) - 1)


def roll(x, shift):
    size = x.shape[1]
    shift = shift % size
    return x if shift == 0 else pltpu.roll(x, shift, 1)


def stacked(x):
    high = x.astype(BF16).astype(F32)
    zeros = jnp.zeros((8, x.shape[1]), F32)
    return jnp.concatenate([high, high, x - high, zeros], axis=0).astype(BF16)


def packed_left(ref, block, x):
    high = x.astype(BF16).astype(F32)
    base = block * 128
    ref[:, base : base + 40] = high
    ref[:, base + 40 : base + 80] = x - high
    ref[:, base + 80 : base + 120] = high


def to_partners(even, upward, downward):
    return jnp.where(even, upward, downward), jnp.where(even, downward, upward)


def from_partners(axis, count, first, second):
    index = lax.axis_index(axis)
    even = index % 2 == 0
    above = jnp.where(even, first, second)
    below = jnp.where(even, second, first)
    zeros = jnp.zeros_like(above)
    return jnp.where(index < count - 1, above, zeros), jnp.where(index > 0, below, zeros)


def fine_ends_kernel(rhs, send_a, send_b, sems):
    upward = jnp.where(lax.axis_index("narrow") % 2 == 0, 15, 0)
    copies = [
        pltpu.make_async_copy(rhs.at[:, upward], send_a, sems.at[0]),
        pltpu.make_async_copy(rhs.at[:, 15 - upward], send_b, sems.at[1]),
    ]
    for copy in copies:
        copy.start()
    for copy in copies:
        copy.wait()


def fine_solve_kernel(
    planes, skel, elim, update, solution_out, skeleton, cat, packed, solver, left_c, left_u, turned
):
    left_c[...] = jnp.zeros_like(left_c)
    left_u[...] = jnp.zeros_like(left_u)
    packed_left(left_c, 0, jnp.concatenate([elim[...], skel[...]], axis=0))
    solve = left_c[...].astype(BF16)
    solver[...] = solve
    for x in range(4):
        for part in range(2):
            turned[part] = planes[x * 256 + part * 128 : x * 256 + (part + 1) * 128, :].T
        for k in range(4):
            vector = jnp.concatenate(
                [turned[part, pl.ds(k, 64, stride=4), :] for part in range(2)], axis=1
            )
            product = dot(solve, stacked(vector[24:64]))
            skeleton[x, :, k * 256 : (k + 1) * 256] = vector[:24] - product[40:64]
            solution_vector = product[:40]
            solution_out[k, x] = solution_vector
            cat[k, x] = stacked(solution_vector)
    for dx in range(3):
        packed_left(left_u, dx, update[dx * 216 : (dx + 1) * 216, :])
    packed[...] = left_u[...].astype(BF16)


def along_z(product, rows, z, last):
    minus, zero, plus = [product[d * rows : (d + 1) * rows] for d in range(3)]
    return (
        zero
        + jnp.where(z > 0, roll(minus, 1), 0.0)
        + jnp.where(z < last, roll(plus, -1), 0.0)
    )


def fine_plane(operator, cat, k, c):
    first = max(0, c - 2)
    last = min(3, c)
    columns = operator[:, (first - c + 2) * 128 : (last - c + 3) * 128]
    right = cat[k, first : last + 1].reshape((last + 1 - first) * 128, 256)
    product = dot(columns, right)
    lane = lanes((24, 256))
    sums = [along_z(product[dy * 72 : (dy + 1) * 72], 24, lane % 16, 15) for dy in range(3)]
    return (
        sums[1]
        + jnp.where(lane >= 16, roll(sums[0], 16), 0.0)
        + jnp.where(lane < 240, roll(sums[2], -16), 0.0)
    )


def fine_outside_kernel(cat, packed, edge):
    operator = packed[...]
    for k in range(4):
        for side, c in ((0, 0), (1, 5)):
            edge[side, :, k * 256 : (k + 1) * 256] = fine_plane(operator, cat, k, c)


def fine_inside_kernel(cat, packed, solution_in, after, skeleton, solved, rest, out_rows):
    operator = packed[...]
    for k in range(4):
        for x in range(4):
            here = slice(k * 256, (k + 1) * 256)
            rest[x, :, here] = skeleton[x, :, here] - fine_plane(operator, cat, k, x + 1)
    for x in range(4):
        for part in range(2):
            for k in range(4):
                out_rows[part, pl.ds(k, 40, stride=4), :] = solution_in[
                    k, x, :, part * 128 : (part + 1) * 128
                ]
            solved[x * 256 + part * 128 : x * 256 + (part + 1) * 128, :] = out_rows[part].T


def fine_border(above, below, k, c):
    half = lanes((24, 128))
    here = slice(k * 128, (k + 1) * 128)
    start = jnp.where(half < 16, roll(below[:, here], -16 * c), 0.0)
    end = jnp.where(half >= 112, roll(above[:, here], 112 - 16 * c), 0.0)
    return start, end


def fine_edge_kernel(
    narrow, edge, packed, solver, got_a, got_b, sum_above, sum_below, send_a, send_b, turned
):
    above, below = from_partners("narrow", narrow, got_a[...], got_b[...])
    turned[...] = jnp.concatenate([below, above], axis=0).T
    vectors = [turned[pl.ds(k, 64, stride=4), :][24:64] for k in range(4)]
    solution_vector = dot(solver[...], stacked(jnp.concatenate(vectors, axis=1)))[:40]
    operator = packed[...]
    half = lanes((40, 128))
    z = lanes((24, 512)) % 16
    sums = []
    for side, base in ((0, 0), (1, 144)):
        blocks = []
        for k in range(4):
            block = roll(solution_vector[:, k * 128 : (k + 1) * 128], 64 * side)
            blocks.append(jnp.where(half < 64, block, 0.0))
        right = []
        for d in range(3):
            moved = [roll(block, 16 * (2 - d)) for block in blocks]
            right.append(stacked(jnp.concatenate(moved, axis=1)))
        product = dot(operator[base : base + 72], jnp.concatenate(right, axis=0))
        sums.append(along_z(product, 24, z, 15))
    below, above = sums
    sum_below[...] = below
    sum_above[...] = above
    even = lax.axis_index("slab") % 2 == 0
    for k in range(4):
        planes = []
        for side, c in ((0, 0), (1, 5)):
            start, end = fine_border(above, below, k, c)
            planes.append(
                (
                    edge[side, :, k * 256 : k * 256 + 128] + start,
                    edge[side, :, k * 256 + 128 : (k + 1) * 256] + end,
                )
            )
        for part in range(2):
            here = slice(k * 256 + part * 128, k * 256 + (part + 1) * 128)
            send_a[:, here], send_b[:, here] = to_partners(even, planes[1][part], planes[0][part])


def operators_mid_kernel(after, skel, elim, update, solve_h, solve_l, update_h, update_l, sort):
    solve_h[...], solve_l[...] = halves(jnp.concatenate([elim[...], skel[...]], axis=0))
    update_h[...], update_l[...] = halves(update[...])
    row = lax.broadcasted_iota(jnp.int32, (256, 256), 0)
    y, z = row // 16, row % 16
    goal = ((y % 2) * 2 + z % 2) * 64 + (y // 2) * 8 + z // 2
    sort[...] = jnp.where(goal == lanes((256, 256)), 1.0, 0.0).astype(BF16)


def operators_coarse_kernel(after, skel, elim, update, solve_h, solve_l, update_h, update_l, sort):
    solve_h[...], solve_l[...] = halves(jnp.concatenate([elim[...], skel[...]], axis=0))
    update_h[...], update_l[...] = halves(update[...])
    row = lax.broadcasted_iota(jnp.int32, (128, 256), 0)
    x, y, z = row // 64, row // 8 % 8, row % 8
    goal = ((x * 2 + y % 2) * 2 + z % 2) * 32 + (y // 2 + 2) * 4 + z // 2
    sort[...] = jnp.where(goal == lanes((128, 256)), 1.0, 0.0).astype(BF16)


def mid_solve_kernel(
    slabs, rest1, above, below, plane_a, plane_b, sort, solve_h, solve_l, update_h, update_l,
    solution_out, skeleton, send_a, send_b,
    parts, vector,
):
    plane_above, plane_below = from_partners("slab", slabs, plane_a[...], plane_b[...])
    for k in range(4):
        for x in range(4):
            start, end = fine_border(above, below, k, x + 1)
            here = slice(k * 256, (k + 1) * 256)
            value = rest1[x, :, here] - jnp.concatenate([start, end], axis=1)
            if x == 0:
                value = value - plane_below[:, here]
            if x == 3:
                value = value - plane_above[:, here]
            top = value.astype(BF16).astype(F32)
            parts[k * 4 + x] = jnp.concatenate([top, value - top], axis=0).astype(BF16)
    arranged = dot(parts[...].reshape(16 * 48, 256), sort[...])
    half = lanes((24, 128))
    for k in range(4):
        for dx in range(2):
            pair = []
            for x in (dx, 2 + dx):
                base = (k * 4 + x) * 48
                pair.append(arranged[base : base + 24] + arranged[base + 24 : base + 48])
            for dy in range(2):
                first, second = [v[:, dy * 128 : (dy + 1) * 128] for v in pair]
                here = slice(k * 128, (k + 1) * 128)
                child = (dx * 2 + dy) * 2
                vector[child * 24 : child * 24 + 24, here] = jnp.where(
                    half < 64, first, roll(second, 64)
                )
                vector[child * 24 + 24 : child * 24 + 48, here] = jnp.where(
                    half < 64, roll(first, 64), second
                )
    result = dot3(solve_h[...], solve_l[...], vector[48:, :])
    solution_vector = result[:144]
    solution_out[...] = solution_vector
    skeleton[...] = vector[:48, :] - result[144:]

    j = lanes((144, 128)) // 8 % 8
    ends = []
    for end, wanted in enumerate((0, 7)):
        total = None
        for k in range(4):
            block = solution_vector[:, k * 128 : (k + 1) * 128]
            for x in range(2):
                u = k * 2 + x
                moved = roll(block, 8 * (u - wanted) - 64 * x + 64 * end)
                total = moved if total is None else jnp.where(j == u, moved, total)
        ends.append(total)
    spot = lanes((48, 128))
    l = spot % 8
    right = jnp.where(lanes((144, 128)) < 64, ends[0], ends[1])
    sums = [[], []]
    for dx in range(3):
        rows = []
        for dy in (2, 0):
            base = (dx * 9 + dy * 3) * 48
            rows.append(slice(base, base + 144))
        both = [dot3(update_h[r, :], update_l[r, :], right) for r in rows]
        for end in range(2):
            sums[end].append(along_z(both[end], 48, l, 7))
    x = spot // 8 % 2
    messages = []
    for end in range(2):
        minus, zero, plus = sums[end]
        inside = zero + jnp.where(x == 0, roll(plus, -8), roll(minus, 8))
        outside = jnp.where(x == 0, plus, minus)
        if end == 0:
            messages.append(jnp.where(spot < 64, inside, roll(outside, 64)))
        else:
            messages.append(jnp.where(spot < 64, roll(inside, 64), outside))
    send_a[...], send_b[...] = to_partners(lax.axis_index("narrow") % 2 == 0, messages[1], messages[0])


def mid_update_kernel(solution_in, skeleton, update_h, update_l, rest, edge, product):
    product[...] = dot3(update_h[...], update_l[...], solution_in[...])
    lane = lanes((48, 128))
    i, j, l = lane // 64, lane // 8 % 8, lane % 8
    for k in range(4):
        here = slice(k * 128, (k + 1) * 128)
        totals = []
        for dx in range(3):
            sums = []
            for dy in range(3):
                base = (dx * 9 + dy * 3) * 48
                sums.append(along_z(product[base : base + 144, here], 48, l, 7))
            totals.append(
                sums[1]
                + jnp.where(j > 0, roll(sums[0], 8), 0.0)
                + jnp.where(j < 7, roll(sums[2], -8), 0.0)
            )
        minus, zero, plus = totals
        inside = zero + jnp.where(i == 0, roll(plus, 64), roll(minus, 64))
        rest[:, here] = skeleton[:, here] - inside
        edge[:, here] = jnp.where(i == 0, plus, minus)


def mid_border(above, below, k, a):
    lane = lanes((48, 128))
    j = lane // 8 % 8
    total = jnp.zeros((48, 128), F32)
    for x in range(2):
        start = a * 64 + (k * 2 + x) * 8
        here = lane // 64 == x
        total = jnp.where(here & (j == 0), roll(below, x * 64 - start), total)
        total = jnp.where(here & (j == 7), roll(above, x * 64 + 56 - start), total)
    return total


def mid_edge_kernel(narrow, edge, got_a, got_b, send_a, send_b):
    above, below = from_partners("narrow", narrow, got_a[...], got_b[...])
    even = lax.axis_index("slab") % 2 == 0
    half = lanes((48, 128))
    for p in range(2):
        pair = []
        for k in (2 * p, 2 * p + 1):
            pair.append(edge[:, k * 128 : (k + 1) * 128] + mid_border(above, below, k, 1))
        moved = roll(pair[0], 64)
        low = jnp.where(half >= 64, moved, pair[1])
        high = jnp.where(half < 64, moved, pair[1])
        here = slice(p * 128, (p + 1) * 128)
        send_a[:, here], send_b[:, here] = to_partners(even, high, low)


def mid_solved_kernel(after, solution_in, solved, out_rows):
    for k in range(4):
        out_rows[pl.ds(k, 144, stride=4), :] = solution_in[:, k * 128 : (k + 1) * 128]
    solved[...] = out_rows[...].T


def coarse_solve_kernel(
    slabs, narrow, rest2, got_a, got_b, plane_a, plane_b, sort, solve_h, solve_l, update_h, update_l,
    solution_out, skeleton, send_a, send_b,
    parts, vector,
):
    above, below = from_partners("narrow", narrow, got_a[...], got_b[...])
    plane_above, plane_below = from_partners("slab", slabs, plane_a[...], plane_b[...])
    half = lanes((48, 128))
    for k in range(4):
        here = slice(k * 128, (k + 1) * 128)
        pack = slice(k // 2 * 128, (k // 2 + 1) * 128)
        up, down = plane_above[:, pack], plane_below[:, pack]
        if k % 2 == 1:
            up, down = roll(up, 64), roll(down, 64)
        value = rest2[:, here] - mid_border(above, below, k, 0) - jnp.where(half < 64, down, up)
        top = value.astype(BF16).astype(F32)
        parts[k] = jnp.concatenate([top, value - top], axis=0).astype(BF16)
    arranged = dot(parts[...].reshape(4 * 96, 128), sort[...])
    for child in range(8):
        total = None
        for k in range(4):
            from_columns = slice(child // 4 * 128, (child // 4 + 1) * 128)
            value = (
                arranged[k * 96 : k * 96 + 48, from_columns]
                + arranged[k * 96 + 48 : k * 96 + 96, from_columns]
            )
            moved = roll(value, 32 * (k - child % 4))
            total = moved if total is None else jnp.where(half // 32 == k, moved, total)
        vector[child * 48 : (child + 1) * 48, :] = total
    result = dot3(solve_h[...], solve_l[...], vector[96:, :])
    solution_vector = result[:288]
    solution_out[...] = solution_vector
    skeleton[...] = vector[:96, :] - result[288:]
    low = coarse_plane(update_h, update_l, solution_vector, 2)
    high = coarse_plane(update_h, update_l, solution_vector, 0)
    send_a[...], send_b[...] = to_partners(lax.axis_index("slab") % 2 == 0, high, low)


def coarse_plane(update_h, update_l, solution_vector, dx):
    sol_h, sol_l = halves(solution_vector)
    rows = slice(dx * 864, (dx + 1) * 864)
    both = dot(update_h[rows, :], jnp.concatenate([sol_h, sol_l], axis=1))
    product = both[:, :128] + both[:, 128:] + dot(update_l[rows, :], sol_h)
    l = lanes((96, 128)) % 4
    total = None
    for dz in range(3):
        column = None
        for dy in range(3):
            base = (dy * 3 + dz) * 96
            moved = roll(product[base : base + 96, :], -((dy - 1) * 4 + dz - 1))
            column = moved if column is None else column + moved
        if dz == 0:
            column = jnp.where(l > 0, column, 0.0)
        if dz == 2:
            column = jnp.where(l < 3, column, 0.0)
        total = column if total is None else total + column
    return total


def coarse_update_kernel(after, solution_in, skeleton, update_h, update_l, solved, rest, out_rows):
    solution_vector = solution_in[...]
    rest[...] = skeleton[...] - coarse_plane(update_h, update_l, solution_vector, 1)
    for k in range(4):
        out_rows[pl.ds(k, 288, stride=4), :] = roll(solution_vector, -32 * k)
    columns = out_rows[...].T
    for y in range(4):
        solved[y] = columns[8 + y * 4 : 12 + y * 4, :]


def coarse_edge_kernel(slabs, rest, plane_a, plane_b, out, rows):
    above, below = from_partners("slab", slabs, plane_a[...], plane_b[...])
    value = rest[...] - above - below
    for k in range(4):
        rows[pl.ds(k, 96, stride=4), :] = roll(value, -32 * k)
    out[...] = rows[...].T[4:28, :]


def join_kernel(*refs):
    for i, block in enumerate(refs[:-1]):
        refs[-1][i * 24 : (i + 1) * 24, :] = block[...]


def gather_kernel(chips, own, other, out, rows):
    mine = lax.axis_index("narrow")
    rows[...] = jnp.zeros_like(rows)
    for distance in range(chips):
        for parity, blocks in enumerate((own, other)):
            base = pl.multiple_of((mine ^ (distance * 2 + parity)) * 16, 8)
            here = pl.ds(base, 24)
            rows[here, :] = rows[here, :] + blocks[distance * 24 : (distance + 1) * 24, :]
    for y in range(chips * 8):
        out[y] = rows[4 + y * 4 : 8 + y * 4, :]


def call(kernel, operands, outs, scratch=(), flops=0, unread=(), where=pltpu.VMEM, sems=0):
    vmem = pl.BlockSpec(memory_space=pltpu.VMEM)
    out_shape = [jax.ShapeDtypeStruct(shape, dtype) for shape, dtype in outs]
    moved = sum(
        x.size * x.dtype.itemsize
        for x in [v for i, v in enumerate(operands) if i not in unread] + out_shape
    )
    specs = [
        pl.BlockSpec(memory_space=pl.ANY if i in unread else where) for i in range(len(operands))
    ]
    scratch_shapes = [pltpu.VMEM(shape, dtype) for shape, dtype in scratch]
    if sems:
        scratch_shapes.append(pltpu.SemaphoreType.DMA((sems,)))
    return pl.pallas_call(
        kernel,
        out_shape=out_shape,
        in_specs=specs,
        out_specs=[vmem] * len(outs),
        scratch_shapes=scratch_shapes,
        compiler_params=pltpu.CompilerParams(vmem_limit_bytes=VMEM_LIMIT),
        cost_estimate=pl.CostEstimate(flops=flops, bytes_accessed=moved, transcendentals=0),
    )(*operands)


def swap_narrow(first, second):
    count = lax.axis_size("narrow")
    pairs = [[(i, (i + 1 if i % 2 == parity else i - 1) % count) for i in range(count)] for parity in (0, 1)]
    return [lax.ppermute(value, "narrow", pair) for value, pair in zip((first, second), pairs)]


def swap_slab(first, second):
    slabs, narrow = lax.axis_size("slab"), lax.axis_size("narrow")
    results = []
    for parity, value in enumerate((first, second)):
        pairs = []
        for i in range(slabs):
            j = i + 1 if i % 2 == parity else i - 1
            for n in range(narrow):
                other = j * narrow + n if 0 <= j < slabs else i * narrow + (n ^ 1)
                pairs.append((i * narrow + n, other))
        results.append(lax.ppermute(value, ("slab", "narrow"), pairs))
    return results


def local(rhs, skel1, elim1, update1, skel2, elim2, update2, skel3, elim3, update3):
    slabs, narrow = lax.axis_size("slab"), lax.axis_size("narrow")

    got_a, got_b = swap_narrow(
        *call(
            fine_ends_kernel,
            [pltpu.with_memory_space_constraint(rhs, pltpu.HBM)],
            [((4, 16, 256), F32)] * 2,
            flops=1 << 31,
            where=pltpu.HBM,
            sems=2,
        )
    )
    solution1, skeleton, cat, packed, solver = call(
        fine_solve_kernel,
        [rhs.reshape(1024, 256), skel1, elim1, update1.reshape(648, 40)],
        [
            ((4, 4, 40, 256), F32),
            ((4, 24, 1024), F32),
            ((4, 4, 128, 256), BF16),
            ((216, 384), BF16),
            ((64, 128), BF16),
        ],
        [
            ((64, 128), F32),
            ((216, 384), F32),
            ((2, 256, 128), F32),
        ],
        flops=1 << 29,
    )
    (edge,) = call(fine_outside_kernel, [cat, packed], [((2, 24, 1024), F32)], flops=1 << 30)
    above, below, send_a, send_b = call(
        functools.partial(fine_edge_kernel, narrow),
        [edge, packed, solver, got_a.reshape(64, 256), got_b.reshape(64, 256)],
        [((24, 512), F32)] * 2 + [((24, 1024), F32)] * 2,
        [((256, 128), F32)],
    )
    after = send_a
    plane_a, plane_b = swap_slab(send_a, send_b)
    solved1, rest = call(
        fine_inside_kernel,
        [cat, packed, solution1, send_a, skeleton],
        [((1024, 160), F32), ((4, 24, 1024), F32)],
        [((2, 160, 128), F32)],
        flops=1 << 30,
        unread=(3,),
    )
    *solve2, update2_h, update2_l, sort2 = call(
        operators_mid_kernel,
        [send_a, skel2, elim2, update2.reshape(1296, 144)],
        [((192, 144), BF16)] * 2 + [((1296, 144), BF16)] * 2 + [((256, 256), BF16)],
        unread=(0,),
    )

    solution2, skeleton, send_a, send_b = call(
        functools.partial(mid_solve_kernel, slabs),
        [rest, above, below, plane_a, plane_b, sort2, *solve2, update2_h, update2_l],
        [((144, 512), F32), ((48, 512), F32), ((48, 128), F32), ((48, 128), F32)],
        [((16, 48, 256), BF16), ((192, 512), F32)],
        flops=1 << 29,
    )
    got_a, got_b = swap_narrow(send_a, send_b)
    rest, edge = call(
        mid_update_kernel,
        [solution2, skeleton, update2_h, update2_l],
        [((48, 512), F32), ((48, 512), F32)],
        [((1296, 512), F32)],
        flops=1 << 30,
    )
    send_a, send_b = call(
        functools.partial(mid_edge_kernel, narrow),
        [edge, got_a, got_b],
        [((48, 256), F32)] * 2,
    )
    plane_a, plane_b = swap_slab(send_a, send_b)
    (solved2,) = call(
        mid_solved_kernel,
        [send_a, solution2],
        [((128, 576), F32)],
        [((576, 128), F32)],
        unread=(0,),
    )
    *solve3, update3_h, update3_l, sort3 = call(
        operators_coarse_kernel,
        [after, skel3, elim3, update3.reshape(2592, 288)],
        [((384, 288), BF16)] * 2 + [((2592, 288), BF16)] * 2 + [((128, 256), BF16)],
        unread=(0,),
    )

    solution3, skeleton, send_a, send_b = call(
        functools.partial(coarse_solve_kernel, slabs, narrow),
        [rest, got_a, got_b, plane_a, plane_b, sort3, *solve3, update3_h, update3_l],
        [((288, 128), F32), ((96, 128), F32), ((96, 128), F32), ((96, 128), F32)],
        [((4, 96, 128), BF16), ((384, 128), F32)],
        flops=1 << 29,
    )
    plane_a, plane_b = swap_slab(send_a, send_b)
    solved3, rest = call(
        coarse_update_kernel,
        [send_a, solution3, skeleton, update3_h, update3_l],
        [((4, 4, 1152), F32), ((96, 128), F32)],
        [((1152, 128), F32)],
        flops=1 << 29,
        unread=(0,),
    )
    (mine,) = call(
        functools.partial(coarse_edge_kernel, slabs),
        [rest, plane_a, plane_b],
        [((24, 384), F32)],
        [((384, 128), F32)],
    )
    chips = narrow // 2
    blocks = [mine] + [
        lax.ppermute(mine, "narrow", [(i, i ^ (2 * d)) for i in range(narrow)])
        for d in range(1, chips)
    ]
    (own,) = call(join_kernel, blocks, [((chips * 24, 384), F32)])
    other = lax.ppermute(own, "narrow", [(i, i ^ 1) for i in range(narrow)])
    (coarse,) = call(
        functools.partial(gather_kernel, chips),
        [own, other],
        [((chips * 8, 4, 384), F32)],
        [((chips * 32 + 8, 384), F32)],
    )
    return (
        solved1.reshape(4, 16, 16, 160),
        solved2.reshape(2, 8, 8, 576),
        solved3.reshape(1, 4, 4, 1152),
        coarse.reshape(1, chips * 8, 4, 384),
    )


def solution(mesh):
    return jax.shard_map(
        local,
        mesh=mesh,
        in_specs=(P("slab", "narrow", None, None), P(), P(), P(), P(), P(), P(), P(), P(), P()),
        out_specs=(
            P("slab", "narrow", None, None),
            P("slab", "narrow", None, None),
            P("slab", "narrow", None, None),
            P("slab", None, None, None),
        ),
        check_vma=False,
    )
```

```python
import functools

import jax
import jax.numpy as jnp
from jax import lax
from jax.experimental import pallas as pl
from jax.experimental.pallas import tpu as pltpu
from jax.sharding import PartitionSpec as P

F32 = jnp.float32
BF16 = jnp.bfloat16
VMEM_LIMIT = 20 * 1024 * 1024


def dot(a, b):
    return lax.dot_general(a, b, (((1,), (0,)), ((), ())), preferred_element_type=F32)


def halves(x):
    high = x.astype(BF16)
    return high, (x - high.astype(F32)).astype(BF16)


def dot3(a_high, a_low, b):
    b_high, b_low = halves(b)
    return dot(a_high, b_high) + dot(a_low, b_high) + dot(a_high, b_low)


def lanes(shape):
    return lax.broadcasted_iota(jnp.int32, shape, len(shape) - 1)


def roll(x, shift):
    size = x.shape[1]
    shift = shift % size
    return x if shift == 0 else pltpu.roll(x, shift, 1)


def stacked(x):
    high = x.astype(BF16).astype(F32)
    zeros = jnp.zeros((8, x.shape[1]), F32)
    return jnp.concatenate([high, high, x - high, zeros], axis=0).astype(BF16)


def packed_left(ref, block, x):
    high = x.astype(BF16).astype(F32)
    base = block * 128
    ref[:, base : base + 40] = high
    ref[:, base + 40 : base + 80] = x - high
    ref[:, base + 80 : base + 120] = high


def to_partners(even, upward, downward):
    return jnp.where(even, upward, downward), jnp.where(even, downward, upward)


def from_partners(axis, count, first, second):
    index = lax.axis_index(axis)
    even = index % 2 == 0
    above = jnp.where(even, first, second)
    below = jnp.where(even, second, first)
    zeros = jnp.zeros_like(above)
    return jnp.where(index < count - 1, above, zeros), jnp.where(index > 0, below, zeros)


def fine_ends_kernel(rhs, send_a, send_b, sems):
    upward = jnp.where(lax.axis_index("narrow") % 2 == 0, 13, 0)
    copies = [
        pltpu.make_async_copy(rhs.at[:, pl.ds(upward, 3)], send_a, sems.at[0]),
        pltpu.make_async_copy(rhs.at[:, pl.ds(13 - upward, 3)], send_b, sems.at[1]),
    ]
    for copy in copies:
        copy.start()
    for copy in copies:
        copy.wait()


def fine_solve_kernel(
    planes, skel, elim, update, solution_out, skeleton, cat, packed, solver, left_c, left_u, turned
):
    left_c[...] = jnp.zeros_like(left_c)
    left_u[...] = jnp.zeros_like(left_u)
    packed_left(left_c, 0, jnp.concatenate([elim[...], skel[...]], axis=0))
    solve = left_c[...].astype(BF16)
    solver[...] = solve
    for x in range(4):
        for part in range(2):
            turned[part] = planes[x * 256 + part * 128 : x * 256 + (part + 1) * 128, :].T
        for k in range(4):
            vector = jnp.concatenate(
                [turned[part, pl.ds(k, 64, stride=4), :] for part in range(2)], axis=1
            )
            product = dot(solve, stacked(vector[24:64]))
            skeleton[x, :, k * 256 : (k + 1) * 256] = vector[:24] - product[40:64]
            solution_vector = product[:40]
            solution_out[k, x] = solution_vector
            cat[k, x] = stacked(solution_vector)
    for dx in range(3):
        packed_left(left_u, dx, update[dx * 216 : (dx + 1) * 216, :])
    packed[...] = left_u[...].astype(BF16)


def along_z(product, rows, z, last):
    minus, zero, plus = [product[d * rows : (d + 1) * rows] for d in range(3)]
    return (
        zero
        + jnp.where(z > 0, roll(minus, 1), 0.0)
        + jnp.where(z < last, roll(plus, -1), 0.0)
    )


def fine_plane(operator, cat, k, c):
    first = max(0, c - 2)
    last = min(3, c)
    columns = operator[:, (first - c + 2) * 128 : (last - c + 3) * 128]
    right = cat[k, first : last + 1].reshape((last + 1 - first) * 128, 256)
    product = dot(columns, right)
    lane = lanes((24, 256))
    sums = [along_z(product[dy * 72 : (dy + 1) * 72], 24, lane % 16, 15) for dy in range(3)]
    return (
        sums[1]
        + jnp.where(lane >= 16, roll(sums[0], 16), 0.0)
        + jnp.where(lane < 240, roll(sums[2], -16), 0.0)
    )


def fine_outside_kernel(cat, packed, edge):
    operator = packed[...]
    for k in range(4):
        for side, c in ((0, 0), (1, 5)):
            edge[side, :, k * 256 : (k + 1) * 256] = fine_plane(operator, cat, k, c)


def strip_columns():
    return lanes((24, 512)) // 16 % 8


def strip_outer(j):
    return (j == 1) | (j == 2) | (j == 5) | (j == 6)


def strip_plane(operator, strips, c):
    first = max(0, c - 2)
    last = min(3, c)
    columns = operator[:, (first - c + 2) * 128 : (last - c + 3) * 128]
    right = strips[first : last + 1].reshape((last + 1 - first) * 128, 512)
    product = dot(columns, right)
    z = lanes((24, 512)) % 16
    sums = [along_z(product[dy * 72 : (dy + 1) * 72], 24, z, 15) for dy in range(3)]
    j = strip_columns()
    inner = (j > 0) & (j < 7)
    return (
        jnp.where(strip_outer(j), sums[1], 0.0)
        + jnp.where(inner & (j != 4), roll(sums[0], 16), 0.0)
        + jnp.where(inner & (j != 3), roll(sums[2], -16), 0.0)
    )


def strip_ends(strip, k):
    half = lanes((24, 128))
    here = strip[:, k * 128 : (k + 1) * 128]
    return (
        jnp.where(half < 16, roll(here, -48), 0.0),
        jnp.where(half >= 112, roll(here, 48), 0.0),
    )


def fine_edge_kernel(
    narrow, after, edge, packed, solver, solution_in, got_a, got_b, strips, skeleton, send_a, send_b, turned
):
    above, below = from_partners("narrow", narrow, got_a[...], got_b[...])
    j = lanes((40, 512)) // 16 % 8
    for x in range(4):
        here = slice(x * 48, (x + 1) * 48)
        rows = [below[here], jnp.zeros((32, 256), F32), above[here]]
        turned[...] = jnp.concatenate(rows, axis=0).T
        vectors = [turned[pl.ds(k, 64, stride=4), :] for k in range(4)]
        vector = jnp.concatenate(vectors, axis=1)
        product = dot(solver[...], stacked(vector[24:64]))
        skeleton[x] = vector[:24] - product[40:64]
        own = [solution_in[k, x] for k in range(4)]
        starts = jnp.concatenate([roll(v[:, :128], 48) for v in own], axis=1)
        ends = jnp.concatenate([roll(v[:, 128:], -48) for v in own], axis=1)
        strips[x] = stacked(jnp.where(j == 3, starts, jnp.where(j == 4, ends, product[:40])))
    operator = packed[...]
    even = lax.axis_index("slab") % 2 == 0
    outer = strip_outer(lanes((24, 128)) // 16)
    sides = [strip_plane(operator, strips, c) for c in (0, 5)]
    for k in range(4):
        for part in range(2):
            here = slice(k * 256 + part * 128, k * 256 + (part + 1) * 128)
            low, high = [edge[i, :, here] + strip_ends(sides[i], k)[part] for i in range(2)]
            send_a[:, here], send_b[:, here] = to_partners(even, high, low)
    for p in range(2):
        low, high = [
            jnp.where(
                outer,
                v[:, p * 256 : p * 256 + 128],
                roll(v[:, p * 256 + 128 : (p + 1) * 256], 32),
            )
            for v in sides
        ]
        here = slice(1024 + p * 128, 1152 + p * 128)
        send_a[:, here], send_b[:, here] = to_partners(even, high, low)


def fine_inside_kernel(cat, packed, solution_in, skeleton, solved, rest, out_rows):
    operator = packed[...]
    for k in range(4):
        for x in range(4):
            here = slice(k * 256, (k + 1) * 256)
            rest[x, :, here] = skeleton[x, :, here] - fine_plane(operator, cat, k, x + 1)
    for x in range(4):
        for part in range(2):
            for k in range(4):
                out_rows[part, pl.ds(k, 40, stride=4), :] = solution_in[
                    k, x, :, part * 128 : (part + 1) * 128
                ]
            solved[x * 256 + part * 128 : x * 256 + (part + 1) * 128, :] = out_rows[part].T


def fine_strip_kernel(packed, after, inner, strips, strip_skeleton, rest, strip_rest):
    operator = packed[...]
    for x in range(4):
        strip = strip_plane(operator, strips, x + 1)
        strip_rest[x] = strip_skeleton[x] - strip
        for k in range(4):
            here = slice(k * 256, (k + 1) * 256)
            rest[x, :, here] = inner[x, :, here] - jnp.concatenate(strip_ends(strip, k), axis=1)


def operators_mid_kernel(
    after, skel, elim, update, solve_h, solve_l, update_h, update_l, sort, sort_strip
):
    solve_h[...], solve_l[...] = halves(jnp.concatenate([elim[...], skel[...]], axis=0))
    update_h[...], update_l[...] = halves(update[...])
    row = lax.broadcasted_iota(jnp.int32, (256, 256), 0)
    y, z = row // 16, row % 16
    goal = ((y % 2) * 2 + z % 2) * 64 + (y // 2) * 8 + z // 2
    sort[...] = jnp.where(goal == lanes((256, 256)), 1.0, 0.0).astype(BF16)
    row = lax.broadcasted_iota(jnp.int32, (128, 512), 0)
    j, z = row // 16, row % 16
    goal = (((j + 1) % 2) * 2 + z % 2) * 128 + j // 4 * 64 + z // 2
    goal = jnp.where(strip_outer(j) & (j < 4), ((j - 1) * 2 + z % 2) * 128 + z // 2, goal)
    wanted = strip_outer(j) & (goal == lanes((128, 512)))
    sort_strip[...] = jnp.where(wanted, 1.0, 0.0).astype(BF16)


def operators_coarse_kernel(after, skel, elim, update, solve_h, solve_l, update_h, update_l, sort):
    solve_h[...], solve_l[...] = halves(jnp.concatenate([elim[...], skel[...]], axis=0))
    update_h[...], update_l[...] = halves(update[...])
    row = lax.broadcasted_iota(jnp.int32, (128, 256), 0)
    x, y, z = row // 64, row // 8 % 8, row % 8
    goal = ((x * 2 + y % 2) * 2 + z % 2) * 32 + (y // 2 + 2) * 4 + z // 2
    sort[...] = jnp.where(goal == lanes((128, 256)), 1.0, 0.0).astype(BF16)


def mid_solve_kernel(
    slabs, narrow, rest1, strip_rest, plane_a, plane_b, sort, sort_strip,
    solve_h, solve_l, update_h, update_l,
    solution_out, skeleton, sum_above, sum_below,
    parts, strip_parts, vector,
):
    plane_above, plane_below = from_partners("slab", slabs, plane_a[...], plane_b[...])
    index = lax.axis_index("narrow")
    column = lanes((24, 128)) // 16
    first, end = jnp.where(index > 0, 0, 4), jnp.where(index < narrow - 1, 8, 4)
    there = strip_outer(column) & (column >= first) & (column < end)
    for k in range(4):
        for x in range(4):
            here = slice(k * 256, (k + 1) * 256)
            value = rest1[x, :, here]
            strip = strip_rest[x, :, k * 128 : (k + 1) * 128]
            if x in (0, 3):
                plane = plane_below if x == 0 else plane_above
                value = value - plane[:, here]
                outside = plane[:, 1024 + k // 2 * 128 : 1152 + k // 2 * 128]
                strip = strip - (roll(outside, -32) if k % 2 == 1 else outside)
            strip = jnp.where(there, strip, 0.0)
            top = value.astype(BF16).astype(F32)
            parts[k * 4 + x] = jnp.concatenate([top, value - top], axis=0).astype(BF16)
            top = strip.astype(BF16).astype(F32)
            strip_parts[k * 4 + x] = jnp.concatenate([top, strip - top], axis=0).astype(BF16)
    arranged = dot(parts[...].reshape(16 * 48, 256), sort[...])
    strip_arranged = dot(strip_parts[...].reshape(16 * 48, 128), sort_strip[...])
    for child in range(2, 8):
        dx, group = divmod(child, 4)
        total = None
        for k in range(4):
            for i in range(2):
                base = (k * 4 + i * 2 + dx) * 48
                columns = slice(group * 128, (group + 1) * 128)
                piece = (
                    strip_arranged[base : base + 24, columns]
                    + strip_arranged[base + 24 : base + 48, columns]
                )
                moved = roll(piece, (k * 2 + i) * 8)
                total = moved if total is None else total + moved
        vector[child * 24 : child * 24 + 24, 512:] = total
    half = lanes((24, 128))
    for k in range(4):
        for dx in range(2):
            pair = []
            for x in (dx, 2 + dx):
                base = (k * 4 + x) * 48
                pair.append(arranged[base : base + 24] + arranged[base + 24 : base + 48])
            for dy in range(2):
                first, second = [v[:, dy * 128 : (dy + 1) * 128] for v in pair]
                here = slice(k * 128, (k + 1) * 128)
                child = (dx * 2 + dy) * 2
                vector[child * 24 : child * 24 + 24, here] = jnp.where(
                    half < 64, first, roll(second, 64)
                )
                vector[child * 24 + 24 : child * 24 + 48, here] = jnp.where(
                    half < 64, roll(first, 64), second
                )
    result = dot3(solve_h[...], solve_l[...], vector[48:, :])
    solution_out[...] = result[:144, :512]
    skeleton[...] = vector[:48, :512] - result[144:, :512]
    right = result[:144, 512:]
    spot = lanes((48, 128))
    l = spot % 8
    sums = [[], []]
    for dx in range(3):
        rows = []
        for dy in (0, 2):
            base = (dx * 9 + dy * 3) * 48
            rows.append(slice(base, base + 144))
        both = [dot3(update_h[r, :], update_l[r, :], right) for r in rows]
        for end in range(2):
            sums[end].append(along_z(both[end], 48, l, 7))
    x = spot // 8 % 2
    messages = []
    for end in range(2):
        minus, zero, plus = sums[end]
        inside = zero + jnp.where(x == 0, roll(plus, -8), roll(minus, 8))
        outside = jnp.where(x == 0, plus, minus)
        if end == 0:
            messages.append(jnp.where(spot < 64, inside, roll(outside, 64)))
        else:
            messages.append(jnp.where(spot < 64, roll(inside, 64), outside))
    sum_below[...], sum_above[...] = messages


def mid_plane(update_h, update_l, solution_vector, dx, product):
    rows = slice(dx * 432, (dx + 1) * 432)
    product[...] = dot3(update_h[rows, :], update_l[rows, :], solution_vector)
    lane = lanes((48, 128))
    j, l = lane // 8 % 8, lane % 8
    totals = []
    for k in range(4):
        here = slice(k * 128, (k + 1) * 128)
        sums = [along_z(product[dy * 144 : (dy + 1) * 144, here], 48, l, 7) for dy in range(3)]
        totals.append(
            sums[1]
            + jnp.where(j > 0, roll(sums[0], 8), 0.0)
            + jnp.where(j < 7, roll(sums[2], -8), 0.0)
        )
    return totals


def mid_outside_kernel(
    solution_in, skeleton, above, below, update_h, update_l, partial, send_a, send_b, product
):
    minus = mid_plane(update_h, update_l, solution_in[...], 0, product.at[0])
    plus = mid_plane(update_h, update_l, solution_in[...], 2, product.at[1])
    half = lanes((48, 128))
    edges = []
    for k in range(4):
        here = slice(k * 128, (k + 1) * 128)
        partial[:, here] = skeleton[:, here] - jnp.where(
            half < 64, roll(plus[k], 64), roll(minus[k], 64)
        )
        edges.append(jnp.where(half < 64, plus[k], minus[k]) + mid_border(above, below, k, 1))
    even = lax.axis_index("slab") % 2 == 0
    for p in range(2):
        moved = roll(edges[2 * p], 64)
        low = jnp.where(half >= 64, moved, edges[2 * p + 1])
        high = jnp.where(half < 64, moved, edges[2 * p + 1])
        here = slice(p * 128, (p + 1) * 128)
        send_a[:, here], send_b[:, here] = to_partners(even, high, low)


def mid_inside_kernel(after, solution_in, partial, above, below, update_h, update_l, rest, product):
    zero = mid_plane(update_h, update_l, solution_in[...], 1, product)
    for k in range(4):
        here = slice(k * 128, (k + 1) * 128)
        rest[:, here] = partial[:, here] - zero[k] - mid_border(above, below, k, 0)


def mid_border(above, below, k, a):
    lane = lanes((48, 128))
    j = lane // 8 % 8
    total = jnp.zeros((48, 128), F32)
    for x in range(2):
        start = a * 64 + (k * 2 + x) * 8
        here = lane // 64 == x
        total = jnp.where(here & (j == 0), roll(below[...], x * 64 - start), total)
        total = jnp.where(here & (j == 7), roll(above[...], x * 64 + 56 - start), total)
    return total


def mid_solved_kernel(after, solution_in, solved, out_rows):
    for k in range(4):
        out_rows[pl.ds(k, 144, stride=4), :] = solution_in[:, k * 128 : (k + 1) * 128]
    solved[...] = out_rows[...].T


def coarse_solve_kernel(
    slabs, rest2, plane_a, plane_b, sort, solve_h, solve_l, update_h, update_l,
    solution_out, skeleton, send_a, send_b,
    parts, vector,
):
    plane_above, plane_below = from_partners("slab", slabs, plane_a[...], plane_b[...])
    half = lanes((48, 128))
    for k in range(4):
        here = slice(k * 128, (k + 1) * 128)
        pack = slice(k // 2 * 128, (k // 2 + 1) * 128)
        up, down = plane_above[:, pack], plane_below[:, pack]
        if k % 2 == 1:
            up, down = roll(up, 64), roll(down, 64)
        value = rest2[:, here] - jnp.where(half < 64, down, up)
        top = value.astype(BF16).astype(F32)
        parts[k] = jnp.concatenate([top, value - top], axis=0).astype(BF16)
    arranged = dot(parts[...].reshape(4 * 96, 128), sort[...])
    for child in range(8):
        total = None
        for k in range(4):
            from_columns = slice(child // 4 * 128, (child // 4 + 1) * 128)
            value = (
                arranged[k * 96 : k * 96 + 48, from_columns]
                + arranged[k * 96 + 48 : k * 96 + 96, from_columns]
            )
            moved = roll(value, 32 * (k - child % 4))
            total = moved if total is None else jnp.where(half // 32 == k, moved, total)
        vector[child * 48 : (child + 1) * 48, :] = total
    result = dot3(solve_h[...], solve_l[...], vector[96:, :])
    solution_vector = result[:288]
    solution_out[...] = solution_vector
    skeleton[...] = vector[:96, :] - result[288:]
    low = coarse_plane(update_h, update_l, solution_vector, 2)
    high = coarse_plane(update_h, update_l, solution_vector, 0)
    send_a[...], send_b[...] = to_partners(lax.axis_index("slab") % 2 == 0, high, low)


def coarse_plane(update_h, update_l, solution_vector, dx):
    sol_h, sol_l = halves(solution_vector)
    rows = slice(dx * 864, (dx + 1) * 864)
    both = dot(update_h[rows, :], jnp.concatenate([sol_h, sol_l], axis=1))
    product = both[:, :128] + both[:, 128:] + dot(update_l[rows, :], sol_h)
    l = lanes((96, 128)) % 4
    total = None
    for dz in range(3):
        column = None
        for dy in range(3):
            base = (dy * 3 + dz) * 96
            moved = roll(product[base : base + 96, :], -((dy - 1) * 4 + dz - 1))
            column = moved if column is None else column + moved
        if dz == 0:
            column = jnp.where(l > 0, column, 0.0)
        if dz == 2:
            column = jnp.where(l < 3, column, 0.0)
        total = column if total is None else total + column
    return total


def coarse_update_kernel(after, solution_in, skeleton, update_h, update_l, solved, rest, out_rows):
    solution_vector = solution_in[...]
    rest[...] = skeleton[...] - coarse_plane(update_h, update_l, solution_vector, 1)
    for k in range(4):
        out_rows[pl.ds(k, 288, stride=4), :] = roll(solution_vector, -32 * k)
    columns = out_rows[...].T
    for y in range(4):
        solved[y] = columns[8 + y * 4 : 12 + y * 4, :]


def coarse_edge_kernel(slabs, rest, plane_a, plane_b, out, rows):
    above, below = from_partners("slab", slabs, plane_a[...], plane_b[...])
    value = rest[...] - above - below
    for k in range(4):
        rows[pl.ds(k, 96, stride=4), :] = roll(value, -32 * k)
    out[...] = rows[...].T[4:28, :]


def join_kernel(*refs):
    for i, block in enumerate(refs[:-1]):
        refs[-1][i * 24 : (i + 1) * 24, :] = block[...]


def gather_kernel(chips, own, other, out, rows):
    mine = lax.axis_index("narrow")
    rows[...] = jnp.zeros_like(rows)
    for distance in range(chips):
        for parity, blocks in enumerate((own, other)):
            base = pl.multiple_of((mine ^ (distance * 2 + parity)) * 16, 8)
            here = pl.ds(base, 24)
            rows[here, :] = rows[here, :] + blocks[distance * 24 : (distance + 1) * 24, :]
    for y in range(chips * 8):
        out[y] = rows[4 + y * 4 : 8 + y * 4, :]


def call(kernel, operands, outs, scratch=(), flops=0, unread=(), where=pltpu.VMEM, sems=0):
    vmem = pl.BlockSpec(memory_space=pltpu.VMEM)
    out_shape = [jax.ShapeDtypeStruct(shape, dtype) for shape, dtype in outs]
    moved = sum(
        x.size * x.dtype.itemsize
        for x in [v for i, v in enumerate(operands) if i not in unread] + out_shape
    )
    specs = [
        pl.BlockSpec(memory_space=pl.ANY if i in unread else where) for i in range(len(operands))
    ]
    scratch_shapes = [pltpu.VMEM(shape, dtype) for shape, dtype in scratch]
    if sems:
        scratch_shapes.append(pltpu.SemaphoreType.DMA((sems,)))
    return pl.pallas_call(
        kernel,
        out_shape=out_shape,
        in_specs=specs,
        out_specs=[vmem] * len(outs),
        scratch_shapes=scratch_shapes,
        compiler_params=pltpu.CompilerParams(vmem_limit_bytes=VMEM_LIMIT),
        cost_estimate=pl.CostEstimate(flops=flops, bytes_accessed=moved, transcendentals=0),
    )(*operands)


def swap_narrow(first, second):
    count = lax.axis_size("narrow")
    pairs = [[(i, (i + 1 if i % 2 == parity else i - 1) % count) for i in range(count)] for parity in (0, 1)]
    return [lax.ppermute(value, "narrow", pair) for value, pair in zip((first, second), pairs)]


def swap_slab(first, second):
    slabs, narrow = lax.axis_size("slab"), lax.axis_size("narrow")
    results = []
    for parity, value in enumerate((first, second)):
        pairs = []
        for i in range(slabs):
            j = i + 1 if i % 2 == parity else i - 1
            for n in range(narrow):
                other = j * narrow + n if 0 <= j < slabs else i * narrow + (n ^ 1)
                pairs.append((i * narrow + n, other))
        results.append(lax.ppermute(value, ("slab", "narrow"), pairs))
    return results


def local(rhs, skel1, elim1, update1, skel2, elim2, update2, skel3, elim3, update3):
    slabs, narrow = lax.axis_size("slab"), lax.axis_size("narrow")

    got_a, got_b = swap_narrow(
        *call(
            fine_ends_kernel,
            [pltpu.with_memory_space_constraint(rhs, pltpu.HBM)],
            [((4, 3, 16, 256), F32)] * 2,
            flops=1 << 31,
            where=pltpu.HBM,
            sems=2,
        )
    )
    solution1, skeleton, cat, packed, solver = call(
        fine_solve_kernel,
        [rhs.reshape(1024, 256), skel1, elim1, update1.reshape(648, 40)],
        [
            ((4, 4, 40, 256), F32),
            ((4, 24, 1024), F32),
            ((4, 4, 128, 256), BF16),
            ((216, 384), BF16),
            ((64, 128), BF16),
        ],
        [
            ((64, 128), F32),
            ((216, 384), F32),
            ((2, 256, 128), F32),
        ],
        flops=1 << 29,
    )
    (edge,) = call(fine_outside_kernel, [cat, packed], [((2, 24, 1024), F32)], flops=1 << 30)
    solved1, inner = call(
        fine_inside_kernel,
        [cat, packed, solution1, skeleton],
        [((1024, 160), F32), ((4, 24, 1024), F32)],
        [((2, 160, 128), F32)],
        flops=1 << 30,
    )
    strips, strip_skeleton, send_a, send_b = call(
        functools.partial(fine_edge_kernel, narrow),
        [inner, edge, packed, solver, solution1, got_a.reshape(192, 256), got_b.reshape(192, 256)],
        [((4, 128, 512), BF16), ((4, 24, 512), F32)] + [((24, 1280), F32)] * 2,
        [((256, 128), F32)],
        unread=(0,),
    )
    after = send_a
    plane_a, plane_b = swap_slab(send_a, send_b)
    rest, strip_rest = call(
        fine_strip_kernel,
        [packed, send_a, inner, strips, strip_skeleton],
        [((4, 24, 1024), F32), ((4, 24, 512), F32)],
        flops=1 << 29,
        unread=(1,),
    )
    *solve2, update2_h, update2_l, sort2, sort_strip = call(
        operators_mid_kernel,
        [send_a, skel2, elim2, update2.reshape(1296, 144)],
        [((192, 144), BF16)] * 2
        + [((1296, 144), BF16)] * 2
        + [((256, 256), BF16), ((128, 512), BF16)],
        unread=(0,),
    )

    solution2, skeleton, above, below = call(
        functools.partial(mid_solve_kernel, slabs, narrow),
        [rest, strip_rest, plane_a, plane_b, sort2, sort_strip, *solve2, update2_h, update2_l],
        [((144, 512), F32), ((48, 512), F32), ((48, 128), F32), ((48, 128), F32)],
        [((16, 48, 256), BF16), ((16, 48, 128), BF16), ((192, 640), F32)],
        flops=1 << 29,
    )
    partial, send_a, send_b = call(
        mid_outside_kernel,
        [solution2, skeleton, above, below, update2_h, update2_l],
        [((48, 512), F32), ((48, 256), F32), ((48, 256), F32)],
        [((2, 432, 512), F32)],
        flops=1 << 29,
    )
    plane_a, plane_b = swap_slab(send_a, send_b)
    (rest,) = call(
        mid_inside_kernel,
        [send_a, solution2, partial, above, below, update2_h, update2_l],
        [((48, 512), F32)],
        [((432, 512), F32)],
        flops=1 << 29,
        unread=(0,),
    )
    (solved2,) = call(
        mid_solved_kernel,
        [send_a, solution2],
        [((128, 576), F32)],
        [((576, 128), F32)],
        unread=(0,),
    )
    *solve3, update3_h, update3_l, sort3 = call(
        operators_coarse_kernel,
        [send_a, skel3, elim3, update3.reshape(2592, 288)],
        [((384, 288), BF16)] * 2 + [((2592, 288), BF16)] * 2 + [((128, 256), BF16)],
        unread=(0,),
    )

    solution3, skeleton, send_a, send_b = call(
        functools.partial(coarse_solve_kernel, slabs),
        [rest, plane_a, plane_b, sort3, *solve3, update3_h, update3_l],
        [((288, 128), F32), ((96, 128), F32), ((96, 128), F32), ((96, 128), F32)],
        [((4, 96, 128), BF16), ((384, 128), F32)],
        flops=1 << 29,
    )
    plane_a, plane_b = swap_slab(send_a, send_b)
    solved3, rest = call(
        coarse_update_kernel,
        [send_a, solution3, skeleton, update3_h, update3_l],
        [((4, 4, 1152), F32), ((96, 128), F32)],
        [((1152, 128), F32)],
        flops=1 << 29,
        unread=(0,),
    )
    (mine,) = call(
        functools.partial(coarse_edge_kernel, slabs),
        [rest, plane_a, plane_b],
        [((24, 384), F32)],
        [((384, 128), F32)],
    )
    chips = narrow // 2
    blocks = [mine] + [
        lax.ppermute(mine, "narrow", [(i, i ^ (2 * d)) for i in range(narrow)])
        for d in range(1, chips)
    ]
    (own,) = call(join_kernel, blocks, [((chips * 24, 384), F32)])
    other = lax.ppermute(own, "narrow", [(i, i ^ 1) for i in range(narrow)])
    (coarse,) = call(
        functools.partial(gather_kernel, chips),
        [own, other],
        [((chips * 8, 4, 384), F32)],
        [((chips * 32 + 8, 384), F32)],
    )
    return (
        solved1.reshape(4, 16, 16, 160),
        solved2.reshape(2, 8, 8, 576),
        solved3.reshape(1, 4, 4, 1152),
        coarse.reshape(1, chips * 8, 4, 384),
    )


def solution(mesh):
    return jax.shard_map(
        local,
        mesh=mesh,
        in_specs=(P("slab", "narrow", None, None), P(), P(), P(), P(), P(), P(), P(), P(), P()),
        out_specs=(
            P("slab", "narrow", None, None),
            P("slab", "narrow", None, None),
            P("slab", "narrow", None, None),
            P("slab", None, None, None),
        ),
        check_vma=False,
    )
```

```python
import functools

import jax
import jax.numpy as jnp
from jax import lax
from jax.experimental import pallas as pl
from jax.experimental.pallas import tpu as pltpu
from jax.sharding import PartitionSpec as P

F32 = jnp.float32
BF16 = jnp.bfloat16
VMEM_LIMIT = 20 * 1024 * 1024


def dot(a, b):
    return lax.dot_general(a, b, (((1,), (0,)), ((), ())), preferred_element_type=F32)


def halves(x):
    high = x.astype(BF16)
    return high, (x - high.astype(F32)).astype(BF16)


def dot3(a_high, a_low, b):
    b_high, b_low = halves(b)
    return dot(a_high, b_high) + dot(a_low, b_high) + dot(a_high, b_low)


def dot3_narrow(a_high, a_low, b):
    b_high, b_low = halves(b)
    both = dot(a_high, jnp.concatenate([b_high, b_low], axis=1))
    return both[:, :128] + both[:, 128:] + dot(a_low, b_high)


def lanes(shape):
    return lax.broadcasted_iota(jnp.int32, shape, len(shape) - 1)


def roll(x, shift):
    size = x.shape[1]
    shift = shift % size
    return x if shift == 0 else pltpu.roll(x, shift, 1)


def stacked(x):
    high = x.astype(BF16).astype(F32)
    zeros = jnp.zeros((8, x.shape[1]), F32)
    return jnp.concatenate([high, high, x - high, zeros], axis=0).astype(BF16)


def packed_left(ref, block, x):
    high = x.astype(BF16).astype(F32)
    base = block * 128
    ref[:, base : base + 40] = high
    ref[:, base + 40 : base + 80] = x - high
    ref[:, base + 80 : base + 120] = high


def to_partners(even, upward, downward):
    return jnp.where(even, upward, downward), jnp.where(even, downward, upward)


def from_partners(axis, count, first, second):
    index = lax.axis_index(axis)
    even = index % 2 == 0
    above = jnp.where(even, first, second)
    below = jnp.where(even, second, first)
    zeros = jnp.zeros_like(above)
    return jnp.where(index < count - 1, above, zeros), jnp.where(index > 0, below, zeros)


def fine_ends_kernel(rhs, send_a, send_b, sems):
    upward = jnp.where(lax.axis_index("narrow") % 2 == 0, 13, 0)
    copies = []
    for x in range(4):
        for side, (start, out) in enumerate(((upward, send_a), (13 - upward, send_b))):
            copies.append(
                pltpu.make_async_copy(
                    rhs.at[x, pl.ds(start, 3)], out.at[x], sems.at[x * 2 + side]
                )
            )
    for copy in copies:
        copy.start()
    for copy in copies:
        copy.wait()


def fine_solve_kernel(
    planes, skel, elim, update, solution_out, skeleton, cat, packed, solver, left_c, left_u, turned
):
    left_c[...] = jnp.zeros_like(left_c)
    left_u[...] = jnp.zeros_like(left_u)
    packed_left(left_c, 0, jnp.concatenate([elim[...], skel[...]], axis=0))
    solve = left_c[...].astype(BF16)
    solver[...] = solve
    for x in range(4):
        for part in range(2):
            turned[part] = planes[x * 256 + part * 128 : x * 256 + (part + 1) * 128, :].T
        for k in range(4):
            vector = jnp.concatenate(
                [turned[part, pl.ds(k, 64, stride=4), :] for part in range(2)], axis=1
            )
            product = dot(solve, stacked(vector[24:64]))
            skeleton[x, :, k * 256 : (k + 1) * 256] = vector[:24] - product[40:64]
            solution_vector = product[:40]
            solution_out[k, x] = solution_vector
            cat[k, x] = stacked(solution_vector)
    for dx in range(3):
        packed_left(left_u, dx, update[dx * 216 : (dx + 1) * 216, :])
    packed[...] = left_u[...].astype(BF16)


def along_z(product, rows, z, last):
    minus, zero, plus = [product[d * rows : (d + 1) * rows] for d in range(3)]
    return (
        zero
        + jnp.where(z > 0, roll(minus, 1), 0.0)
        + jnp.where(z < last, roll(plus, -1), 0.0)
    )


def fine_plane(operator, cat, k, c):
    first = max(0, c - 2)
    last = min(3, c)
    columns = operator[:, (first - c + 2) * 128 : (last - c + 3) * 128]
    right = cat[k, first : last + 1].reshape((last + 1 - first) * 128, 256)
    product = dot(columns, right)
    lane = lanes((24, 256))
    sums = [along_z(product[dy * 72 : (dy + 1) * 72], 24, lane % 16, 15) for dy in range(3)]
    return (
        sums[1]
        + jnp.where(lane >= 16, roll(sums[0], 16), 0.0)
        + jnp.where(lane < 240, roll(sums[2], -16), 0.0)
    )


def fine_outside_kernel(cat, packed, edge):
    operator = packed[...]
    for k in range(4):
        for side, c in ((0, 0), (1, 5)):
            edge[side, :, k * 256 : (k + 1) * 256] = fine_plane(operator, cat, k, c)


def strip_columns():
    return lanes((24, 512)) // 16 % 8


def strip_outer(j):
    return (j == 1) | (j == 2) | (j == 5) | (j == 6)


def strip_plane(operator, strips, c):
    first = max(0, c - 2)
    last = min(3, c)
    columns = operator[:, (first - c + 2) * 128 : (last - c + 3) * 128]
    right = strips[first : last + 1].reshape((last + 1 - first) * 128, 512)
    product = dot(columns, right)
    z = lanes((24, 512)) % 16
    sums = [along_z(product[dy * 72 : (dy + 1) * 72], 24, z, 15) for dy in range(3)]
    j = strip_columns()
    inner = (j > 0) & (j < 7)
    return (
        jnp.where(strip_outer(j), sums[1], 0.0)
        + jnp.where(inner & (j != 4), roll(sums[0], 16), 0.0)
        + jnp.where(inner & (j != 3), roll(sums[2], -16), 0.0)
    )


def strip_ends(strip, k):
    half = lanes((24, 128))
    here = strip[:, k * 128 : (k + 1) * 128]
    return (
        jnp.where(half < 16, roll(here, -48), 0.0),
        jnp.where(half >= 112, roll(here, 48), 0.0),
    )


def fine_edge_kernel(
    narrow, after, edge, packed, solver, solution_in, got_a, got_b, strips, skeleton, send_a, send_b, turned
):
    above, below = from_partners("narrow", narrow, got_a[...], got_b[...])
    j = lanes((40, 512)) // 16 % 8
    for x in range(4):
        here = slice(x * 48, (x + 1) * 48)
        rows = [below[here], jnp.zeros((32, 256), F32), above[here]]
        turned[...] = jnp.concatenate(rows, axis=0).T
        vectors = [turned[pl.ds(k, 64, stride=4), :] for k in range(4)]
        vector = jnp.concatenate(vectors, axis=1)
        product = dot(solver[...], stacked(vector[24:64]))
        skeleton[x] = vector[:24] - product[40:64]
        own = [solution_in[k, x] for k in range(4)]
        starts = jnp.concatenate([roll(v[:, :128], 48) for v in own], axis=1)
        ends = jnp.concatenate([roll(v[:, 128:], -48) for v in own], axis=1)
        strips[x] = stacked(jnp.where(j == 3, starts, jnp.where(j == 4, ends, product[:40])))
    operator = packed[...]
    even = lax.axis_index("slab") % 2 == 0
    outer = strip_outer(lanes((24, 128)) // 16)
    sides = [strip_plane(operator, strips, c) for c in (0, 5)]
    for k in range(4):
        for part in range(2):
            here = slice(k * 256 + part * 128, k * 256 + (part + 1) * 128)
            low, high = [edge[i, :, here] + strip_ends(sides[i], k)[part] for i in range(2)]
            send_a[:, here], send_b[:, here] = to_partners(even, high, low)
    for p in range(2):
        low, high = [
            jnp.where(
                outer,
                v[:, p * 256 : p * 256 + 128],
                roll(v[:, p * 256 + 128 : (p + 1) * 256], 32),
            )
            for v in sides
        ]
        here = slice(1024 + p * 128, 1152 + p * 128)
        send_a[:, here], send_b[:, here] = to_partners(even, high, low)


def fine_inside_kernel(cat, packed, solution_in, skeleton, solved, rest, out_rows):
    operator = packed[...]
    for k in range(4):
        for x in range(4):
            here = slice(k * 256, (k + 1) * 256)
            rest[x, :, here] = skeleton[x, :, here] - fine_plane(operator, cat, k, x + 1)
    for x in range(4):
        for part in range(2):
            for k in range(4):
                out_rows[part, pl.ds(k, 40, stride=4), :] = solution_in[
                    k, x, :, part * 128 : (part + 1) * 128
                ]
            solved[x * 256 + part * 128 : x * 256 + (part + 1) * 128, :] = out_rows[part].T


def fine_strip_kernel(packed, after, inner, strips, strip_skeleton, rest, strip_rest):
    operator = packed[...]
    for x in range(4):
        strip = strip_plane(operator, strips, x + 1)
        strip_rest[x] = strip_skeleton[x] - strip
        for k in range(4):
            here = slice(k * 256, (k + 1) * 256)
            rest[x, :, here] = inner[x, :, here] - jnp.concatenate(strip_ends(strip, k), axis=1)


def operators_mid_kernel(
    after, skel, elim, update, solve_h, solve_l, update_h, update_l, sort, sort_strip
):
    solve_h[...], solve_l[...] = halves(jnp.concatenate([elim[...], skel[...]], axis=0))
    update_h[...], update_l[...] = halves(update[...])
    row = lax.broadcasted_iota(jnp.int32, (256, 256), 0)
    y, z = row // 16, row % 16
    goal = ((y % 2) * 2 + z % 2) * 64 + (y // 2) * 8 + z // 2
    sort[...] = jnp.where(goal == lanes((256, 256)), 1.0, 0.0).astype(BF16)
    row = lax.broadcasted_iota(jnp.int32, (128, 512), 0)
    j, z = row // 16, row % 16
    goal = (((j + 1) % 2) * 2 + z % 2) * 128 + j // 4 * 64 + z // 2
    goal = jnp.where(strip_outer(j) & (j < 4), ((j - 1) * 2 + z % 2) * 128 + z // 2, goal)
    wanted = strip_outer(j) & (goal == lanes((128, 512)))
    sort_strip[...] = jnp.where(wanted, 1.0, 0.0).astype(BF16)


def operators_coarse_kernel(after, skel, elim, update, solve_h, solve_l, update_h, update_l, sort):
    solve_h[...], solve_l[...] = halves(jnp.concatenate([elim[...], skel[...]], axis=0))
    update_h[...], update_l[...] = halves(update[...])
    row = lax.broadcasted_iota(jnp.int32, (128, 256), 0)
    x, y, z = row // 64, row // 8 % 8, row % 8
    goal = ((x * 2 + y % 2) * 2 + z % 2) * 32 + (y // 2 + 2) * 4 + z // 2
    sort[...] = jnp.where(goal == lanes((128, 256)), 1.0, 0.0).astype(BF16)


def mid_solve_kernel(
    slabs, narrow, rest1, strip_rest, plane_a, plane_b, sort, sort_strip,
    solve_h, solve_l, update_h, update_l,
    solution_out, skeleton, sum_above, sum_below,
    parts, strip_parts, vector,
):
    plane_above, plane_below = from_partners("slab", slabs, plane_a[...], plane_b[...])
    index = lax.axis_index("narrow")
    column = lanes((24, 128)) // 16
    first, end = jnp.where(index > 0, 0, 4), jnp.where(index < narrow - 1, 8, 4)
    there = strip_outer(column) & (column >= first) & (column < end)
    for k in range(4):
        for x in range(4):
            here = slice(k * 256, (k + 1) * 256)
            value = rest1[x, :, here]
            strip = strip_rest[x, :, k * 128 : (k + 1) * 128]
            if x in (0, 3):
                plane = plane_below if x == 0 else plane_above
                value = value - plane[:, here]
                outside = plane[:, 1024 + k // 2 * 128 : 1152 + k // 2 * 128]
                strip = strip - (roll(outside, -32) if k % 2 == 1 else outside)
            strip = jnp.where(there, strip, 0.0)
            top = value.astype(BF16).astype(F32)
            parts[k * 4 + x] = jnp.concatenate([top, value - top], axis=0).astype(BF16)
            top = strip.astype(BF16).astype(F32)
            strip_parts[k * 4 + x] = jnp.concatenate([top, strip - top], axis=0).astype(BF16)
    arranged = dot(parts[...].reshape(16 * 48, 256), sort[...])
    strip_arranged = dot(strip_parts[...].reshape(16 * 48, 128), sort_strip[...])
    for child in range(2, 8):
        dx, group = divmod(child, 4)
        total = None
        for k in range(4):
            for i in range(2):
                base = (k * 4 + i * 2 + dx) * 48
                columns = slice(group * 128, (group + 1) * 128)
                piece = (
                    strip_arranged[base : base + 24, columns]
                    + strip_arranged[base + 24 : base + 48, columns]
                )
                moved = roll(piece, (k * 2 + i) * 8)
                total = moved if total is None else total + moved
        vector[child * 24 : child * 24 + 24, 512:] = total
    half = lanes((24, 128))
    for k in range(4):
        for dx in range(2):
            pair = []
            for x in (dx, 2 + dx):
                base = (k * 4 + x) * 48
                pair.append(arranged[base : base + 24] + arranged[base + 24 : base + 48])
            for dy in range(2):
                first, second = [v[:, dy * 128 : (dy + 1) * 128] for v in pair]
                here = slice(k * 128, (k + 1) * 128)
                child = (dx * 2 + dy) * 2
                vector[child * 24 : child * 24 + 24, here] = jnp.where(
                    half < 64, first, roll(second, 64)
                )
                vector[child * 24 + 24 : child * 24 + 48, here] = jnp.where(
                    half < 64, roll(first, 64), second
                )
    result = dot3(solve_h[...], solve_l[...], vector[48:, :])
    solution_out[...] = result[:144, :512]
    skeleton[...] = vector[:48, :512] - result[144:, :512]
    right = result[:144, 512:]
    spot = lanes((48, 128))
    l = spot % 8
    sums = [[], []]
    for dx in range(3):
        rows = []
        for dy in (0, 2):
            base = (dx * 9 + dy * 3) * 48
            rows.append(slice(base, base + 144))
        both = [dot3_narrow(update_h[r, :], update_l[r, :], right) for r in rows]
        for end in range(2):
            sums[end].append(along_z(both[end], 48, l, 7))
    x = spot // 8 % 2
    messages = []
    for end in range(2):
        minus, zero, plus = sums[end]
        inside = zero + jnp.where(x == 0, roll(plus, -8), roll(minus, 8))
        outside = jnp.where(x == 0, plus, minus)
        if end == 0:
            messages.append(jnp.where(spot < 64, inside, roll(outside, 64)))
        else:
            messages.append(jnp.where(spot < 64, roll(inside, 64), outside))
    sum_below[...], sum_above[...] = messages


def mid_plane(update_h, update_l, solution_vector, dx, product):
    rows = slice(dx * 432, (dx + 1) * 432)
    product[...] = dot3(update_h[rows, :], update_l[rows, :], solution_vector)
    lane = lanes((48, 128))
    j, l = lane // 8 % 8, lane % 8
    totals = []
    for k in range(4):
        here = slice(k * 128, (k + 1) * 128)
        sums = [along_z(product[dy * 144 : (dy + 1) * 144, here], 48, l, 7) for dy in range(3)]
        totals.append(
            sums[1]
            + jnp.where(j > 0, roll(sums[0], 8), 0.0)
            + jnp.where(j < 7, roll(sums[2], -8), 0.0)
        )
    return totals


def mid_outside_kernel(
    solution_in, skeleton, above, below, update_h, update_l, partial, send_a, send_b, product
):
    minus = mid_plane(update_h, update_l, solution_in[...], 0, product.at[0])
    plus = mid_plane(update_h, update_l, solution_in[...], 2, product.at[1])
    half = lanes((48, 128))
    edges = []
    for k in range(4):
        here = slice(k * 128, (k + 1) * 128)
        partial[:, here] = skeleton[:, here] - jnp.where(
            half < 64, roll(plus[k], 64), roll(minus[k], 64)
        )
        edges.append(jnp.where(half < 64, plus[k], minus[k]) + mid_border(above, below, k, 1))
    even = lax.axis_index("slab") % 2 == 0
    for p in range(2):
        moved = roll(edges[2 * p], 64)
        low = jnp.where(half >= 64, moved, edges[2 * p + 1])
        high = jnp.where(half < 64, moved, edges[2 * p + 1])
        here = slice(p * 128, (p + 1) * 128)
        send_a[:, here], send_b[:, here] = to_partners(even, high, low)


def mid_inside_kernel(after, solution_in, partial, above, below, update_h, update_l, rest, product):
    zero = mid_plane(update_h, update_l, solution_in[...], 1, product)
    for k in range(4):
        here = slice(k * 128, (k + 1) * 128)
        rest[:, here] = partial[:, here] - zero[k] - mid_border(above, below, k, 0)


def mid_border(above, below, k, a):
    lane = lanes((48, 128))
    j = lane // 8 % 8
    total = jnp.zeros((48, 128), F32)
    for x in range(2):
        start = a * 64 + (k * 2 + x) * 8
        here = lane // 64 == x
        total = jnp.where(here & (j == 0), roll(below[...], x * 64 - start), total)
        total = jnp.where(here & (j == 7), roll(above[...], x * 64 + 56 - start), total)
    return total


def mid_solved_kernel(after, solution_in, solved, out_rows):
    for k in range(4):
        out_rows[pl.ds(k, 144, stride=4), :] = solution_in[:, k * 128 : (k + 1) * 128]
    solved[...] = out_rows[...].T


def coarse_solve_kernel(
    slabs, rest2, plane_a, plane_b, sort, solve_h, solve_l, update_h, update_l,
    solution_out, skeleton, send_a, send_b,
    parts, vector,
):
    plane_above, plane_below = from_partners("slab", slabs, plane_a[...], plane_b[...])
    half = lanes((48, 128))
    for k in range(4):
        here = slice(k * 128, (k + 1) * 128)
        pack = slice(k // 2 * 128, (k // 2 + 1) * 128)
        up, down = plane_above[:, pack], plane_below[:, pack]
        if k % 2 == 1:
            up, down = roll(up, 64), roll(down, 64)
        value = rest2[:, here] - jnp.where(half < 64, down, up)
        top = value.astype(BF16).astype(F32)
        parts[k] = jnp.concatenate([top, value - top], axis=0).astype(BF16)
    arranged = dot(parts[...].reshape(4 * 96, 128), sort[...])
    for child in range(8):
        total = None
        for k in range(4):
            from_columns = slice(child // 4 * 128, (child // 4 + 1) * 128)
            value = (
                arranged[k * 96 : k * 96 + 48, from_columns]
                + arranged[k * 96 + 48 : k * 96 + 96, from_columns]
            )
            moved = roll(value, 32 * (k - child % 4))
            total = moved if total is None else jnp.where(half // 32 == k, moved, total)
        vector[child * 48 : (child + 1) * 48, :] = total
    result = dot3_narrow(solve_h[...], solve_l[...], vector[96:, :])
    solution_vector = result[:288]
    solution_out[...] = solution_vector
    skeleton[...] = vector[:96, :] - result[288:]
    low = coarse_plane(update_h, update_l, solution_vector, 2)
    high = coarse_plane(update_h, update_l, solution_vector, 0)
    send_a[...], send_b[...] = to_partners(lax.axis_index("slab") % 2 == 0, high, low)


def coarse_plane(update_h, update_l, solution_vector, dx):
    sol_h, sol_l = halves(solution_vector)
    rows = slice(dx * 864, (dx + 1) * 864)
    both = dot(update_h[rows, :], jnp.concatenate([sol_h, sol_l], axis=1))
    product = both[:, :128] + both[:, 128:] + dot(update_l[rows, :], sol_h)
    l = lanes((96, 128)) % 4
    total = None
    for dz in range(3):
        column = None
        for dy in range(3):
            base = (dy * 3 + dz) * 96
            moved = roll(product[base : base + 96, :], -((dy - 1) * 4 + dz - 1))
            column = moved if column is None else column + moved
        if dz == 0:
            column = jnp.where(l > 0, column, 0.0)
        if dz == 2:
            column = jnp.where(l < 3, column, 0.0)
        total = column if total is None else total + column
    return total


def coarse_update_kernel(after, solution_in, skeleton, update_h, update_l, solved, rest, out_rows):
    solution_vector = solution_in[...]
    rest[...] = skeleton[...] - coarse_plane(update_h, update_l, solution_vector, 1)
    for k in range(4):
        out_rows[pl.ds(k, 288, stride=4), :] = roll(solution_vector, -32 * k)
    columns = out_rows[...].T
    for y in range(4):
        solved[y] = columns[8 + y * 4 : 12 + y * 4, :]


def coarse_edge_kernel(slabs, rest, plane_a, plane_b, out, rows):
    above, below = from_partners("slab", slabs, plane_a[...], plane_b[...])
    value = rest[...] - above - below
    for k in range(4):
        rows[pl.ds(k, 96, stride=4), :] = roll(value, -32 * k)
    out[...] = rows[...].T[4:28, :]


def join_kernel(*refs):
    for i, block in enumerate(refs[:-1]):
        refs[-1][i * 24 : (i + 1) * 24, :] = block[...]


def gather_kernel(chips, own, other, out, rows):
    mine = lax.axis_index("narrow")
    rows[...] = jnp.zeros_like(rows)
    for distance in range(chips):
        for parity, blocks in enumerate((own, other)):
            base = pl.multiple_of((mine ^ (distance * 2 + parity)) * 16, 8)
            here = pl.ds(base, 24)
            rows[here, :] = rows[here, :] + blocks[distance * 24 : (distance + 1) * 24, :]
    for y in range(chips * 8):
        out[y] = rows[4 + y * 4 : 8 + y * 4, :]


def call(kernel, operands, outs, scratch=(), flops=0, unread=(), where=pltpu.VMEM, sems=0):
    vmem = pl.BlockSpec(memory_space=pltpu.VMEM)
    out_shape = [jax.ShapeDtypeStruct(shape, dtype) for shape, dtype in outs]
    moved = sum(
        x.size * x.dtype.itemsize
        for x in [v for i, v in enumerate(operands) if i not in unread] + out_shape
    )
    specs = [
        pl.BlockSpec(memory_space=pl.ANY if i in unread else where) for i in range(len(operands))
    ]
    scratch_shapes = [pltpu.VMEM(shape, dtype) for shape, dtype in scratch]
    if sems:
        scratch_shapes.append(pltpu.SemaphoreType.DMA((sems,)))
    return pl.pallas_call(
        kernel,
        out_shape=out_shape,
        in_specs=specs,
        out_specs=[vmem] * len(outs),
        scratch_shapes=scratch_shapes,
        compiler_params=pltpu.CompilerParams(vmem_limit_bytes=VMEM_LIMIT),
        cost_estimate=pl.CostEstimate(flops=flops, bytes_accessed=moved, transcendentals=0),
    )(*operands)


def swap_narrow(first, second):
    count = lax.axis_size("narrow")
    pairs = [[(i, (i + 1 if i % 2 == parity else i - 1) % count) for i in range(count)] for parity in (0, 1)]
    return [lax.ppermute(value, "narrow", pair) for value, pair in zip((first, second), pairs)]


def swap_slab(first, second):
    slabs, narrow = lax.axis_size("slab"), lax.axis_size("narrow")
    results = []
    for parity, value in enumerate((first, second)):
        pairs = []
        for i in range(slabs):
            j = i + 1 if i % 2 == parity else i - 1
            for n in range(narrow):
                other = j * narrow + n if 0 <= j < slabs else i * narrow + (n ^ 1)
                pairs.append((i * narrow + n, other))
        results.append(lax.ppermute(value, ("slab", "narrow"), pairs))
    return results


def local(rhs, skel1, elim1, update1, skel2, elim2, update2, skel3, elim3, update3):
    slabs, narrow = lax.axis_size("slab"), lax.axis_size("narrow")

    got_a, got_b = swap_narrow(
        *call(
            fine_ends_kernel,
            [pltpu.with_memory_space_constraint(rhs, pltpu.HBM)],
            [((4, 3, 16, 256), F32)] * 2,
            flops=1 << 31,
            where=pltpu.HBM,
            sems=8,
        )
    )
    solution1, skeleton, cat, packed, solver = call(
        fine_solve_kernel,
        [rhs.reshape(1024, 256), skel1, elim1, update1.reshape(648, 40)],
        [
            ((4, 4, 40, 256), F32),
            ((4, 24, 1024), F32),
            ((4, 4, 128, 256), BF16),
            ((216, 384), BF16),
            ((64, 128), BF16),
        ],
        [
            ((64, 128), F32),
            ((216, 384), F32),
            ((2, 256, 128), F32),
        ],
        flops=1 << 29,
    )
    (edge,) = call(fine_outside_kernel, [cat, packed], [((2, 24, 1024), F32)], flops=1 << 30)
    solved1, inner = call(
        fine_inside_kernel,
        [cat, packed, solution1, skeleton],
        [((1024, 160), F32), ((4, 24, 1024), F32)],
        [((2, 160, 128), F32)],
        flops=1 << 30,
    )
    strips, strip_skeleton, send_a, send_b = call(
        functools.partial(fine_edge_kernel, narrow),
        [inner, edge, packed, solver, solution1, got_a.reshape(192, 256), got_b.reshape(192, 256)],
        [((4, 128, 512), BF16), ((4, 24, 512), F32)] + [((24, 1280), F32)] * 2,
        [((256, 128), F32)],
        unread=(0,),
    )
    after = send_a
    plane_a, plane_b = swap_slab(send_a, send_b)
    rest, strip_rest = call(
        fine_strip_kernel,
        [packed, send_a, inner, strips, strip_skeleton],
        [((4, 24, 1024), F32), ((4, 24, 512), F32)],
        flops=1 << 29,
        unread=(1,),
    )
    *solve2, update2_h, update2_l, sort2, sort_strip = call(
        operators_mid_kernel,
        [send_a, skel2, elim2, update2.reshape(1296, 144)],
        [((192, 144), BF16)] * 2
        + [((1296, 144), BF16)] * 2
        + [((256, 256), BF16), ((128, 512), BF16)],
        unread=(0,),
    )

    solution2, skeleton, above, below = call(
        functools.partial(mid_solve_kernel, slabs, narrow),
        [rest, strip_rest, plane_a, plane_b, sort2, sort_strip, *solve2, update2_h, update2_l],
        [((144, 512), F32), ((48, 512), F32), ((48, 128), F32), ((48, 128), F32)],
        [((16, 48, 256), BF16), ((16, 48, 128), BF16), ((192, 640), F32)],
        flops=1 << 29,
    )
    partial, send_a, send_b = call(
        mid_outside_kernel,
        [solution2, skeleton, above, below, update2_h, update2_l],
        [((48, 512), F32), ((48, 256), F32), ((48, 256), F32)],
        [((2, 432, 512), F32)],
        flops=1 << 29,
    )
    plane_a, plane_b = swap_slab(send_a, send_b)
    (rest,) = call(
        mid_inside_kernel,
        [send_a, solution2, partial, above, below, update2_h, update2_l],
        [((48, 512), F32)],
        [((432, 512), F32)],
        flops=1 << 29,
        unread=(0,),
    )
    (solved2,) = call(
        mid_solved_kernel,
        [send_a, solution2],
        [((128, 576), F32)],
        [((576, 128), F32)],
        unread=(0,),
    )
    *solve3, update3_h, update3_l, sort3 = call(
        operators_coarse_kernel,
        [send_a, skel3, elim3, update3.reshape(2592, 288)],
        [((384, 288), BF16)] * 2 + [((2592, 288), BF16)] * 2 + [((128, 256), BF16)],
        unread=(0,),
    )

    solution3, skeleton, send_a, send_b = call(
        functools.partial(coarse_solve_kernel, slabs),
        [rest, plane_a, plane_b, sort3, *solve3, update3_h, update3_l],
        [((288, 128), F32), ((96, 128), F32), ((96, 128), F32), ((96, 128), F32)],
        [((4, 96, 128), BF16), ((384, 128), F32)],
        flops=1 << 29,
    )
    plane_a, plane_b = swap_slab(send_a, send_b)
    solved3, rest = call(
        coarse_update_kernel,
        [send_a, solution3, skeleton, update3_h, update3_l],
        [((4, 4, 1152), F32), ((96, 128), F32)],
        [((1152, 128), F32)],
        flops=1 << 29,
        unread=(0,),
    )
    (mine,) = call(
        functools.partial(coarse_edge_kernel, slabs),
        [rest, plane_a, plane_b],
        [((24, 384), F32)],
        [((384, 128), F32)],
    )
    chips = narrow // 2
    blocks = [mine] + [
        lax.ppermute(mine, "narrow", [(i, i ^ (2 * d)) for i in range(narrow)])
        for d in range(1, chips)
    ]
    (own,) = call(join_kernel, blocks, [((chips * 24, 384), F32)])
    other = lax.ppermute(own, "narrow", [(i, i ^ 1) for i in range(narrow)])
    (coarse,) = call(
        functools.partial(gather_kernel, chips),
        [own, other],
        [((chips * 8, 4, 384), F32)],
        [((chips * 32 + 8, 384), F32)],
    )
    return (
        solved1.reshape(4, 16, 16, 160),
        solved2.reshape(2, 8, 8, 576),
        solved3.reshape(1, 4, 4, 1152),
        coarse.reshape(1, chips * 8, 4, 384),
    )


def solution(mesh):
    return jax.shard_map(
        local,
        mesh=mesh,
        in_specs=(P("slab", "narrow", None, None), P(), P(), P(), P(), P(), P(), P(), P(), P()),
        out_specs=(
            P("slab", "narrow", None, None),
            P("slab", "narrow", None, None),
            P("slab", "narrow", None, None),
            P("slab", None, None, None),
        ),
        check_vma=False,
    )
```
